256 devices in a mesh: ctx: 16 (over z, core), head: 16 (over y, x).
Axes of the slice: x: 4, y: 4, z: 8, core: 2. Of those that a mesh axis runs over, the one named last changes fastest.
Arguments:
- queries: bfloat16 [16384, 8192], P('ctx', 'head'), may hold values from -0.59765625 to 0.59765625
- keys: bfloat16 [16384, 8192], P('ctx', 'head'), may hold values from -0.59765625 to 0.59765625
- values: bfloat16 [16384, 8192], P('ctx', 'head'), may hold values from -0.59765625 to 0.59765625
- out_grad: bfloat16 [16384, 8192], P(('ctx', 'head')), may hold values from -0.59765625 to 0.59765625
- state_in: float32 [64, 128, 128], P('head'), may hold values from -6 to 6
- exponents: int32 [64], P('head'), may hold values from 1 to 4095, as said below
- boundaries: int32 [8], replicated, may hold values from 1 to 16383
Outputs:
- query_grad: bfloat16 [16384, 8192], P('ctx', 'head')
- key_grad: bfloat16 [16384, 8192], P('ctx', 'head')
- value_grad: bfloat16 [16384, 8192], P('ctx', 'head')
- state_grad: float32 [64, 128, 128], P('head', 'ctx')
The draws below stay inside these ranges and needn't reach their ends.
Inputs may be any that keep to these rules, and one draw needn't show every extreme that they name: `exponents`: each head's exponent is a whole number; larger ones forget faster. `boundaries`: positions may repeat; each occurrence halves the state once more.
All inputs are finite; a program needn't handle non-finite values.
Results may differ from the reference program's by a relative error of at most 0.009.
Values may be sent and summed in bfloat16 or wider, within the bound.
A program may use at most 64 MiB of HBM per device.

```python
import jax
import jax.numpy as jnp
from jax import lax

D_HEAD = 128
BLOCK = 256
BOUNDARY_COUNT = 8
HEADS = 64
SEQUENCE_TOKENS = 16384


def draw_exponents(key, part):
    key = jax.random.fold_in(key, 11)
    first, second, third = jax.random.split(key, 3)
    power = jax.random.randint(first, (HEADS,), 0, 12)
    base = jnp.left_shift(jnp.ones((HEADS,), jnp.int32), power)
    jitter = jnp.remainder(jax.random.randint(second, (HEADS,), 0, 1048576), base)
    drawn = (base + jitter).astype(jnp.int32)
    order = jax.random.permutation(third, HEADS)
    places = jnp.arange(HEADS, dtype=jnp.int32)
    drawn = jnp.where(places == order[0], 4095, drawn)
    drawn = jnp.where(places == order[1], 1, drawn)
    return drawn.astype(jnp.int32)


def touch_ends(values, stream_key, low, largest):
    longest = values.shape.index(max(values.shape))
    spots = []
    for shift in (0, 1):
        where = [jax.random.randint(jax.random.fold_in(stream_key, axis), (), 0, length) for axis, length in enumerate(values.shape)]
        where[longest] = (where[longest] + shift) % values.shape[longest]
        spots.append(tuple(where))
    return values.at[spots[0]].set(low).at[spots[1]].set(largest)


def levels(stream_key, extent, cuts, low, top_value):
    factor_of = 1.0
    for axis_at, blocks in cuts:
        steps = jax.random.uniform(jax.random.fold_in(jax.random.fold_in(stream_key, 6), axis_at), (blocks,), jnp.float32, low / len(cuts), top_value / len(cuts))
        factor_of = factor_of * jnp.repeat(jnp.exp(steps), extent[axis_at] // blocks).reshape((-1,) + (1,) * (len(extent) - 1 - axis_at))
    return factor_of


def noise(own_key, dims, scale, bound, cuts=(), kind=jnp.bfloat16):
    entries = scale * jax.random.normal(own_key, dims, jnp.float32)
    if cuts:
        entries = entries * levels(own_key, dims, cuts, -0.22, 0.18)
    return jnp.clip(entries, -bound, bound).astype(kind)


def setup_inputs(seed: int = 0) -> dict:
    splits = jax.random.split(jax.random.key(seed), 8)
    return {
        "queries": noise(splits[0], (SEQUENCE_TOKENS, HEADS * D_HEAD), 0.09, 0.59765625, ((0, 16), (1, 16))),
        "keys": noise(splits[1], (SEQUENCE_TOKENS, HEADS * D_HEAD), 0.09, 0.59765625, ((0, 16), (1, 16))),
        "values": noise(splits[2], (SEQUENCE_TOKENS, HEADS * D_HEAD), 0.09, 0.59765625, ((0, 16), (1, 16))),
        "out_grad": noise(splits[3], (SEQUENCE_TOKENS, HEADS * D_HEAD), 0.09, 0.59765625, ((0, 256),)),
        "state_in": noise(splits[4], (HEADS, D_HEAD, D_HEAD), 1.0, 6.0, ((0, 16),), jnp.float32),
        "exponents": draw_exponents(jax.random.fold_in(splits[7], 71), 0),
        "boundaries": touch_ends(jax.random.randint(splits[6], (BOUNDARY_COUNT,), 1, SEQUENCE_TOKENS), jax.random.fold_in(splits[6], 1), 1, SEQUENCE_TOKENS - 1).astype(jnp.int32),
    }


def mix(form, left, right):
    return jnp.einsum(form, left, right, precision=lax.Precision.HIGHEST)


def block_rates(exponents, boundaries, start, block, total):
    offsets = jnp.arange(block, dtype=jnp.int32)
    places = start + offsets
    hits = jnp.sum((boundaries[:, None] == places[None, :]).astype(jnp.float32), axis=0)
    linear = (exponents[:, None] * (offsets[None, :] + 1)).astype(jnp.float32) / (4.0 * total)
    return -linear - jnp.cumsum(hits)[None, :]


def block_states(qf, kf, vf, gf, rates):
    head_in = jnp.exp2(rates)[..., None]
    tail_out = jnp.exp2(rates[:, -1:] - rates)[..., None]
    own_state = mix("hjd,hje->hde", kf * tail_out, vf)
    own_grad = mix("hid,hie->hde", qf * head_in, gf)
    return own_state, own_grad, rates[:, -1]


def block_terms(qf, kf, vf, gf, rates, prev_state, following_grad):
    size = rates.shape[1]
    spread = rates[:, :, None] - rates[:, None, :]
    lower = jnp.arange(size)[:, None] >= jnp.arange(size)[None, :]
    weight = jnp.where(lower[None], jnp.exp2(jnp.minimum(spread, 0.0)), 0.0)
    pair_grad = mix("hie,hje->hij", gf, vf) * weight
    pair_key = mix("hid,hjd->hij", qf, kf) * weight
    head_in = jnp.exp2(rates)[..., None]
    tail_out = jnp.exp2(rates[:, -1:] - rates)[..., None]
    dquery = mix("hij,hjd->hid", pair_grad, kf) + head_in * mix("hie,hde->hid", gf, prev_state)
    dkey = mix("hij,hid->hjd", pair_grad, qf) + tail_out * mix("hje,hde->hjd", vf, following_grad)
    dvalue = mix("hij,hie->hje", pair_key, gf) + tail_out * mix("hjd,hde->hje", kf, following_grad)
    return dquery, dkey, dvalue


def heads_first(rows):
    size = rows.shape[0]
    return rows.reshape(size, HEADS, D_HEAD).transpose(1, 0, 2).astype(jnp.float32)


def reference(queries, keys, values, out_grad, state_in, exponents, boundaries):
    count = SEQUENCE_TOKENS // BLOCK
    stacked = tuple(a.reshape(count, BLOCK, HEADS * D_HEAD) for a in (queries, keys, values, out_grad))
    indices = jnp.arange(count, dtype=jnp.int32)

    def forward(state, item):
        index, qb, kb, vb, gb = item
        rates = block_rates(exponents, boundaries, index * BLOCK, BLOCK, SEQUENCE_TOKENS)
        own_state, own_grad, last = block_states(heads_first(qb), heads_first(kb), heads_first(vb), heads_first(gb), rates)
        new_state = jnp.exp2(last)[:, None, None] * state + own_state
        return new_state, (state, own_grad, last)

    _, (prev_states, segment_own_grads, lasts) = lax.scan(forward, state_in, (indices,) + stacked)

    def backward(grad, item):
        own_grad, last = item
        return own_grad + jnp.exp2(last)[:, None, None] * grad, grad

    state_grad, next_grads = lax.scan(backward, jnp.zeros((HEADS, D_HEAD, D_HEAD), jnp.float32), (segment_own_grads, lasts), reverse=True)

    def finish(item):
        index, qb, kb, vb, gb, prev_state, following_grad = item
        rates = block_rates(exponents, boundaries, index * BLOCK, BLOCK, SEQUENCE_TOKENS)
        outs = block_terms(heads_first(qb), heads_first(kb), heads_first(vb), heads_first(gb), rates, prev_state, following_grad)
        return tuple(o.transpose(1, 0, 2).reshape(BLOCK, HEADS * D_HEAD).astype(jnp.bfloat16) for o in outs)

    dquery, dkey, dvalue = lax.map(finish, (indices,) + stacked + (prev_states, next_grads))
    shape = (SEQUENCE_TOKENS, HEADS * D_HEAD)
    return dquery.reshape(shape), dkey.reshape(shape), dvalue.reshape(shape), state_grad
```

```python
import functools

import jax
import jax.numpy as jnp
from jax import lax
from jax.experimental import pallas as pl
from jax.experimental.pallas import tpu as pltpu
from jax.sharding import PartitionSpec as P

D = 128
C = 256
MESH = pl.DeviceIdType.MESH
F32 = jnp.float32
BF16 = jnp.bfloat16
NN = ((1,), (0,))
NT = ((1,), (1,))


def dot(a, b, dims):
    return lax.dot_general(a, b, (dims, ((), ())), preferred_element_type=F32)


def far(step, size):
    return min(step, size - step)


def layer(
    sizes,
    q_hbm, k_hbm, v_hbm, og_hbm, st_hbm, exps, bnds,
    dq_ref, dk_ref, dv_ref, sg_ref,
    q, k, v, g, st, ncol, nrow, tail, hin, w, wt, pk, qh,
    dqi, dki, dvi, prevs, nexts, edge_state,
    fs, fr, fo, fin, fins, bs, br, bo, bin_, bins,
    lsem, gs, gr, fsem, bsem,
):
    heads, chunks, tokens, segments, nbounds, total = sizes
    groups = 16
    ctx = lax.axis_index("ctx")
    me = lax.axis_index("head")
    z, core = ctx // 2, ctx % 2
    y, x = me // 4, me % 4
    rows_each = tokens // groups
    width = heads * D
    srow = D // segments

    head_steps = sorted(
        [(a, b) for a in range(4) for b in range(4) if a or b],
        key=lambda s: -(far(s[0], 4) + far(s[1], 4)),
    )
    ctx_steps = sorted(
        [(a, b) for a in range(segments // 2) for b in range(2) if a or b],
        key=lambda s: -far(s[0], segments // 2),
    )

    def head_peer(step):
        return lax.rem(y + step[0], 4) * 4 + lax.rem(x + step[1], 4)

    def ctx_peer(step):
        return lax.rem(z + step[0], segments // 2) * 2 + lax.rem(core + step[1], 2)

    barrier = pltpu.get_barrier_semaphore()
    for s in head_steps:
        pl.semaphore_signal(barrier, inc=1, device_id=(ctx, head_peer(s)), device_id_type=MESH)
    for s in ctx_steps:
        pl.semaphore_signal(barrier, inc=1, device_id=(ctx_peer(s), me), device_id_type=MESH)

    loads = [
        pltpu.make_async_copy(k_hbm, k, lsem.at[0]),
        pltpu.make_async_copy(v_hbm, v, lsem.at[1]),
        pltpu.make_async_copy(q_hbm, q, lsem.at[2]),
        pltpu.make_async_copy(st_hbm.at[:, pl.ds(pl.multiple_of(ctx * srow, srow), srow), :], st, lsem.at[3]),
    ]
    for c in loads:
        c.start()

    start = ctx * tokens

    def count(t):
        n = jnp.int32(0)
        for b in range(nbounds):
            n = n + jnp.where(bnds[b] <= t, 1, 0)
        return n.astype(F32)

    def rate(h):
        return exps[h].astype(F32) * (1.0 / (4.0 * total))

    def row(value):
        return jnp.exp2(jnp.full((1, D), value, F32))

    def counts(c, _):
        first = start + c * C
        tc = first + lax.broadcasted_iota(jnp.int32, (C, D), 0)
        tr = first + lax.broadcasted_iota(jnp.int32, (8, C), 1)
        nc = jnp.zeros((C, D), F32)
        nr = jnp.zeros((8, C), F32)
        for b in range(nbounds):
            nc = nc + jnp.where(tc >= bnds[b], 1.0, 0.0)
            nr = nr + jnp.where(tr >= bnds[b], 1.0, 0.0)
        ncol[pl.ds(pl.multiple_of(c * C, C), C), :] = nc
        nrow[c] = nr
        return 0

    lax.fori_loop(0, chunks, counts, 0)

    def rates(i, _):
        h, c = i // chunks, lax.rem(i, chunks)
        at = pl.ds(pl.multiple_of(c * C, C), C)
        a = rate(h)
        n = ncol[at, :]
        place = lax.broadcasted_iota(jnp.int32, (C, D), 0).astype(F32)
        before = count(start + c * C - 1)
        after = count(start + c * C + C - 1)
        hin[h, at, :] = jnp.exp2(-a * (place + 1.0) - (n - before))
        tail[h, at, :] = jnp.exp2(-a * ((C - 1.0) - place) - (after - n))
        return 0

    lax.fori_loop(0, heads * chunks, rates, 0)

    pl.semaphore_wait(barrier, len(head_steps) + len(ctx_steps))

    mine = pl.ds(pl.multiple_of(me * rows_each, rows_each), rows_each)
    for h in range(heads):
        at = pl.multiple_of(me * width + h * D, D)
        pltpu.make_async_copy(og_hbm.at[:, pl.ds(at, D)], g.at[mine, pl.ds(h * D, D)], gr.at[h]).start()

    def send_head(h, _):
        for s in head_steps:
            peer = head_peer(s)
            at = pl.multiple_of(peer * width + h * D, D)
            pltpu.make_async_remote_copy(
                src_ref=og_hbm.at[:, pl.ds(at, D)],
                dst_ref=g.at[mine, pl.ds(pl.multiple_of(h * D, D), D)],
                send_sem=gs,
                recv_sem=gr.at[h],
                device_id=(ctx, peer),
                device_id_type=MESH,
            ).start()
        return 0

    lax.fori_loop(0, heads, send_head, 0)

    def exchange(src, dst, ssem, rsem):
        for s in ctx_steps:
            peer = ctx_peer(s)
            pltpu.make_async_remote_copy(
                src_ref=src.at[peer],
                dst_ref=dst.at[ctx],
                send_sem=ssem,
                recv_sem=rsem,
                device_id=(peer, me),
                device_id_type=MESH,
            ).start()
        dst[ctx] = src[ctx]

    def arrived(buf, sem):
        part = buf.at[pl.ds(0, segments - 1)]
        pltpu.make_async_copy(part, part, sem).wait()

    def seg_decay(lo, hi, d):
        a = jnp.concatenate([jnp.full((srow, D), rate(h), F32) for h in range(lo, hi)], axis=0)
        hits = count((d + 1) * tokens - 1) - count(d * tokens - 1)
        return jnp.exp2(-a * float(tokens) - hits)

    def last(h, c):
        hits = count(start + c * C + C - 1) - count(start + c * C - 1)
        return row(-rate(h) * float(C) - hits)

    loads[0].wait()
    loads[1].wait()

    def own_forward(h, _):
        lanes = pl.ds(pl.multiple_of(h * D, D), D)

        def one(c, s):
            at = pl.ds(pl.multiple_of(c * C, C), C)
            kt = (k[at, lanes].astype(F32) * tail[h, at, :]).T.astype(BF16)
            prevs[h, c] = s
            return last(h, c) * s + dot(kt, v[at, lanes], NN)

        edge_state[h] = lax.fori_loop(0, chunks, one, jnp.zeros((D, D), F32))
        return 0

    lax.fori_loop(0, heads, own_forward, 0)

    def stage_forward(j, _):
        at = pl.ds(pl.multiple_of(j * srow, srow), srow)
        fs[j] = edge_state[:, at, :].reshape(heads * srow, D).astype(BF16)
        return 0

    lax.fori_loop(0, segments, stage_forward, 0)
    exchange(fs, fr, fsem.at[0], fsem.at[1])

    loads[2].wait()
    loads[3].wait()

    def prepare(i, _):
        h, c = i // chunks, lax.rem(i, chunks)
        at = pl.ds(pl.multiple_of(c * C, C), C)
        lanes = pl.ds(pl.multiple_of(h * D, D), D)
        a = rate(h)
        n = ncol[at, :]
        nc = jnp.concatenate([n, n], axis=1)
        nr = nrow[c][0:1, :]
        gap = (
            lax.broadcasted_iota(jnp.int32, (C, C), 0) - lax.broadcasted_iota(jnp.int32, (C, C), 1)
        ).astype(F32)
        dn = nc - nr
        w[i] = jnp.where(gap >= 0, jnp.exp2(-a * gap - dn), 0.0)
        weight = jnp.where(gap <= 0, jnp.exp2(a * gap + dn), 0.0)
        wt[i] = weight
        qc = q[at, lanes]
        pk[i] = (dot(k[at, lanes], qc, NT) * weight).astype(BF16)
        qh[i] = (qc.astype(F32) * hin[h, at, :]).T.astype(BF16)
        return 0

    lax.fori_loop(0, heads * chunks, prepare, 0)

    def own_backward(h):
        lanes = pl.ds(h * D, D)
        col = g.at[:, lanes]
        pltpu.make_async_copy(col, col, gr.at[h]).wait()

        def one(i, s):
            c = chunks - 1 - i
            at = pl.ds(pl.multiple_of(c * C, C), C)
            nexts[h, c] = s
            return last(h, c) * s + dot(qh[h * chunks + c], g[at, lanes], NN)

        edge_state[h] = lax.fori_loop(0, chunks, one, jnp.zeros((D, D), F32))

    def send_backward(p):
        def stage(j, _):
            at = pl.ds(pl.multiple_of(j * srow, srow), srow)
            bs[p, j] = edge_state[pl.ds(2 * p, 2), at, :].reshape(2 * srow, D).astype(BF16)
            return 0

        lax.fori_loop(0, segments, stage, 0)
        exchange(bs.at[p], br.at[p], bsem.at[p, 0], bsem.at[p, 1])

    def scan_forward():
        arrived(fr, fsem.at[1])

        def one(d, s):
            fo[d] = s.astype(BF16)
            return seg_decay(0, heads, d) * s + fr[d].astype(F32)

        lax.fori_loop(0, segments, one, st[...].reshape(heads * srow, D))
        exchange(fo, fin, fsem.at[2], fsem.at[3])

    def scan_backward(p):
        arrived(br.at[p], bsem.at[p, 1])

        def one(i, s):
            d = segments - 1 - i
            bo[p, d] = s.astype(BF16)
            return seg_decay(2 * p, 2 * p + 2, d) * s + br[p, d].astype(F32)

        whole = lax.fori_loop(0, segments, one, jnp.zeros((2 * srow, D), F32))
        sg_ref[pl.ds(2 * p, 2)] = whole.reshape(2, srow, D)
        exchange(bo.at[p], bin_.at[p], bsem.at[p, 2], bsem.at[p, 3])

    def inside(h):
        lanes = pl.ds(h * D, D)

        def one(c, _):
            at = pl.ds(pl.multiple_of(c * C, C), C)
            i = h * chunks + c
            gc, vc = g[at, lanes], v[at, lanes]
            grad = (dot(gc, vc, NT) * w[i]).astype(BF16)
            dqi[at, lanes] = dot(grad, k[at, lanes], NN)
            turned = (dot(vc, gc, NT) * wt[i]).astype(BF16)
            dki[at, lanes] = dot(turned, q[at, lanes], NN)
            dvi[at, lanes] = dot(pk[i], gc, NN)
            return 0

        lax.fori_loop(0, chunks, one, 0)

    def finish_query():
        arrived(fin, fsem.at[3])
        got = fin[...].astype(F32)
        for h in range(heads):
            fins[h] = got[:, h * srow:(h + 1) * srow, :].reshape(D, D)

        def one(i, _):
            h, c = i // chunks, lax.rem(i, chunks)
            at = pl.ds(pl.multiple_of(c * C, C), C)
            lanes = pl.ds(pl.multiple_of(h * D, D), D)
            hits = count(start + c * C - 1) - count(start - 1)
            reach = row(-rate(h) * (c * C).astype(F32) - hits)
            state = (prevs[h, c] + reach * fins[h]).astype(BF16)
            dq_ref[at, lanes] = (dqi[at, lanes] + hin[h, at, :] * dot(g[at, lanes], state, NT)).astype(BF16)
            return 0

        lax.fori_loop(0, heads * chunks, one, 0)

    def finish_keys(p):
        arrived(bin_.at[p], bsem.at[p, 3])
        got = bin_[p].astype(F32)
        for e in range(2):
            bins[2 * p + e] = got[:, e * srow:(e + 1) * srow, :].reshape(D, D)

        def one(i, _):
            h, c = 2 * p + i // chunks, lax.rem(i, chunks)
            at = pl.ds(pl.multiple_of(c * C, C), C)
            lanes = pl.ds(pl.multiple_of(h * D, D), D)
            hits = count(start + tokens - 1) - count(start + c * C + C - 1)
            reach = row(-rate(h) * (tokens - C - c * C).astype(F32) - hits)
            grad = (nexts[h, c] + reach * bins[h]).astype(BF16)
            scale = tail[h, at, :]
            dk_ref[at, lanes] = (dki[at, lanes] + scale * dot(v[at, lanes], grad, NT)).astype(BF16)
            dv_ref[at, lanes] = (dvi[at, lanes] + scale * dot(k[at, lanes], grad, NN)).astype(BF16)
            return 0

        lax.fori_loop(0, 2 * chunks, one, 0)

    own_backward(0)
    own_backward(1)
    send_backward(0)
    scan_forward()
    inside(0)
    own_backward(2)
    own_backward(3)
    send_backward(1)
    scan_backward(0)
    inside(1)
    inside(2)
    scan_backward(1)
    inside(3)
    finish_query()
    finish_keys(0)
    finish_keys(1)

    sent = og_hbm.at[:, pl.ds(0, (groups - 1) * width)]
    pltpu.make_async_copy(sent, sent, gs).wait()
    arrived(fs, fsem.at[0])
    arrived(fo, fsem.at[2])
    for p in range(heads // 2):
        arrived(bs.at[p], bsem.at[p, 0])
        arrived(bo.at[p], bsem.at[p, 2])


def store(a, b, c, s, oa, ob, oc, os, sem):
    rows = a.shape[0] // 4
    copies = [pltpu.make_async_copy(s, os, sem.at[12])]
    for i in range(4):
        at = pl.ds(i * rows, rows)
        for j, (src, dst) in enumerate(((a, oa), (b, ob), (c, oc))):
            copies.append(pltpu.make_async_copy(src.at[at], dst.at[at], sem.at[3 * i + j]))
    for copy in copies:
        copy.start()
    for copy in copies:
        copy.wait()


def shards(queries, keys, values, out_grad, state_in, exponents, boundaries):
    tokens, width = queries.shape
    heads = width // D
    chunks = tokens // C
    segments = lax.axis_size("ctx")
    srow = D // segments
    total = tokens * segments
    sizes = (heads, chunks, tokens, segments, boundaries.shape[0], total)
    hbm = pl.BlockSpec(memory_space=pltpu.HBM)
    vmem = pl.BlockSpec(memory_space=pltpu.VMEM)
    smem = pl.BlockSpec(memory_space=pltpu.SMEM)
    n = heads * chunks
    slab = lambda rows: pltpu.VMEM((segments, rows, D), BF16)
    pair = lambda: pltpu.VMEM((heads // 2, segments, 2 * srow, D), BF16)
    results = pl.pallas_call(
        functools.partial(layer, sizes),
        name="layer",
        out_shape=(
            pltpu.VMEM((tokens, width), BF16),
            pltpu.VMEM((tokens, width), BF16),
            pltpu.VMEM((tokens, width), BF16),
            pltpu.VMEM((heads, srow, D), F32),
        ),
        in_specs=[hbm] * 5 + [smem] * 2,
        out_specs=(vmem,) * 4,
        scratch_shapes=[
            pltpu.VMEM((tokens, width), BF16),
            pltpu.VMEM((tokens, width), BF16),
            pltpu.VMEM((tokens, width), BF16),
            pltpu.VMEM((tokens, width), BF16),
            pltpu.VMEM((heads, srow, D), F32),
            pltpu.VMEM((tokens, D), F32),
            pltpu.VMEM((chunks, 8, C), F32),
            pltpu.VMEM((heads, tokens, D), F32),
            pltpu.VMEM((heads, tokens, D), F32),
            pltpu.VMEM((n, C, C), F32),
            pltpu.VMEM((n, C, C), F32),
            pltpu.VMEM((n, C, C), BF16),
            pltpu.VMEM((n, D, C), BF16),
            pltpu.VMEM((tokens, width), F32),
            pltpu.VMEM((tokens, width), F32),
            pltpu.VMEM((tokens, width), F32),
            pltpu.VMEM((heads, chunks, D, D), F32),
            pltpu.VMEM((heads, chunks, D, D), F32),
            pltpu.VMEM((heads, D, D), F32),
            slab(heads * srow),
            slab(heads * srow),
            slab(heads * srow),
            slab(heads * srow),
            pltpu.VMEM((heads, D, D), F32),
            pair(),
            pair(),
            pair(),
            pair(),
            pltpu.VMEM((heads, D, D), F32),
            pltpu.SemaphoreType.DMA((4,)),
            pltpu.SemaphoreType.DMA,
            pltpu.SemaphoreType.DMA((heads,)),
            pltpu.SemaphoreType.DMA((4,)),
            pltpu.SemaphoreType.DMA((heads // 2, 4)),
        ],
        compiler_params=pltpu.CompilerParams(
            collective_id=0, has_side_effects=True, vmem_limit_bytes=48 << 20
        ),
    )(queries, keys, values, out_grad, state_in, exponents, boundaries)
    whole = jax.ShapeDtypeStruct((tokens, width), BF16)
    return pl.pallas_call(
        store,
        name="store",
        out_shape=(whole, whole, whole, jax.ShapeDtypeStruct((heads, srow, D), F32)),
        in_specs=[vmem] * 4,
        out_specs=(hbm,) * 4,
        scratch_shapes=[pltpu.SemaphoreType.DMA((13,))],
    )(*results)


def solution(mesh):
    in_specs = (
        P("ctx", "head"),
        P("ctx", "head"),
        P("ctx", "head"),
        P(("ctx", "head"), None),
        P("head", None, None),
        P("head"),
        P(),
    )
    out_specs = (P("ctx", "head"), P("ctx", "head"), P("ctx", "head"), P("head", "ctx", None))
    return jax.shard_map(shards, mesh=mesh, in_specs=in_specs, out_specs=out_specs, check_vma=False)
```

```python
import functools

import jax
import jax.numpy as jnp
from jax import lax
from jax.experimental import pallas as pl
from jax.experimental.pallas import tpu as pltpu
from jax.sharding import PartitionSpec as P

D = 128
C = 256
MESH = pl.DeviceIdType.MESH
F32 = jnp.float32
BF16 = jnp.bfloat16
NN = ((1,), (0,))
NT = ((1,), (1,))


def dot(a, b, dims):
    return lax.dot_general(a, b, (dims, ((), ())), preferred_element_type=F32)


def far(step, size):
    return min(step, size - step)


def layer(
    sizes,
    q_hbm, k_hbm, v_hbm, og_hbm, st_hbm, exps, bnds,
    dq_ref, dk_ref, dv_ref, sg_ref,
    q, k, v, g, st, ncol, nrow, tail, hin, w, wt, pk, qh,
    dqi, dki, dvi, prevs, nexts, edge_state,
    fs, fr, fo, fin, fins, bs, br, bo, bin_, bins,
    lsem, gs, gr, fsem, bsem,
):
    heads, chunks, tokens, segments, nbounds, total = sizes
    groups = 16
    ctx = lax.axis_index("ctx")
    me = lax.axis_index("head")
    z, core = ctx // 2, ctx % 2
    y, x = me // 4, me % 4
    rows_each = tokens // groups
    width = heads * D
    srow = D // segments

    head_steps = sorted(
        [(a, b) for a in range(4) for b in range(4) if a or b],
        key=lambda s: -(far(s[0], 4) + far(s[1], 4)),
    )
    ctx_steps = sorted(
        [(a, b) for a in range(segments // 2) for b in range(2) if a or b],
        key=lambda s: -far(s[0], segments // 2),
    )

    def head_peer(step):
        return lax.rem(y + step[0], 4) * 4 + lax.rem(x + step[1], 4)

    def ctx_peer(step):
        return lax.rem(z + step[0], segments // 2) * 2 + lax.rem(core + step[1], 2)

    barrier = pltpu.get_barrier_semaphore()
    for s in head_steps:
        pl.semaphore_signal(barrier, inc=1, device_id=(ctx, head_peer(s)), device_id_type=MESH)
    for s in ctx_steps:
        pl.semaphore_signal(barrier, inc=1, device_id=(ctx_peer(s), me), device_id_type=MESH)

    loads = [
        pltpu.make_async_copy(k_hbm, k, lsem.at[0]),
        pltpu.make_async_copy(v_hbm, v, lsem.at[1]),
        pltpu.make_async_copy(q_hbm, q, lsem.at[2]),
        pltpu.make_async_copy(st_hbm.at[:, pl.ds(pl.multiple_of(ctx * srow, srow), srow), :], st, lsem.at[3]),
    ]
    for c in loads:
        c.start()

    start = ctx * tokens

    def count(t):
        n = jnp.int32(0)
        for b in range(nbounds):
            n = n + jnp.where(bnds[b] <= t, 1, 0)
        return n.astype(F32)

    def rate(h):
        return exps[h].astype(F32) * (1.0 / (4.0 * total))

    def row(value):
        return jnp.exp2(jnp.full((1, D), value, F32))

    def counts(c, _):
        first = start + c * C
        tc = first + lax.broadcasted_iota(jnp.int32, (C, D), 0)
        tr = first + lax.broadcasted_iota(jnp.int32, (8, C), 1)
        nc = jnp.zeros((C, D), F32)
        nr = jnp.zeros((8, C), F32)
        for b in range(nbounds):
            nc = nc + jnp.where(tc >= bnds[b], 1.0, 0.0)
            nr = nr + jnp.where(tr >= bnds[b], 1.0, 0.0)
        ncol[pl.ds(pl.multiple_of(c * C, C), C), :] = nc
        nrow[c] = nr
        return 0

    lax.fori_loop(0, chunks, counts, 0)

    def rates(i, _):
        h, c = i // chunks, lax.rem(i, chunks)
        at = pl.ds(pl.multiple_of(c * C, C), C)
        a = rate(h)
        n = ncol[at, :]
        place = lax.broadcasted_iota(jnp.int32, (C, D), 0).astype(F32)
        before = count(start + c * C - 1)
        after = count(start + c * C + C - 1)
        hin[h, at, :] = jnp.exp2(-a * (place + 1.0) - (n - before))
        tail[h, at, :] = jnp.exp2(-a * ((C - 1.0) - place) - (after - n))
        return 0

    lax.fori_loop(0, heads * chunks, rates, 0)

    pl.semaphore_wait(barrier, len(head_steps) + len(ctx_steps))

    mine = pl.ds(pl.multiple_of(me * rows_each, rows_each), rows_each)
    for h in range(heads):
        at = pl.multiple_of(me * width + h * D, D)
        pltpu.make_async_copy(og_hbm.at[:, pl.ds(at, D)], g.at[mine, pl.ds(h * D, D)], gr.at[h]).start()

    def send_head(h, _):
        for s in head_steps:
            peer = head_peer(s)
            at = pl.multiple_of(peer * width + h * D, D)
            pltpu.make_async_remote_copy(
                src_ref=og_hbm.at[:, pl.ds(at, D)],
                dst_ref=g.at[mine, pl.ds(pl.multiple_of(h * D, D), D)],
                send_sem=gs,
                recv_sem=gr.at[h],
                device_id=(ctx, peer),
                device_id_type=MESH,
            ).start()
        return 0

    lax.fori_loop(0, heads, send_head, 0)

    def exchange(src, dst, ssem, rsem):
        for s in ctx_steps:
            peer = ctx_peer(s)
            pltpu.make_async_remote_copy(
                src_ref=src.at[peer],
                dst_ref=dst.at[ctx],
                send_sem=ssem,
                recv_sem=rsem,
                device_id=(peer, me),
                device_id_type=MESH,
            ).start()
        dst[ctx] = src[ctx]

    def arrived(buf, sem):
        part = buf.at[pl.ds(0, segments - 1)]
        pltpu.make_async_copy(part, part, sem).wait()

    def seg_decay(lo, hi, d):
        a = jnp.concatenate([jnp.full((srow, D), rate(h), F32) for h in range(lo, hi)], axis=0)
        hits = count((d + 1) * tokens - 1) - count(d * tokens - 1)
        return jnp.exp2(-a * float(tokens) - hits)

    def last(h, c):
        hits = count(start + c * C + C - 1) - count(start + c * C - 1)
        return row(-rate(h) * float(C) - hits)

    loads[0].wait()
    loads[1].wait()

    def own_forward(h, _):
        lanes = pl.ds(pl.multiple_of(h * D, D), D)

        def one(c, s):
            at = pl.ds(pl.multiple_of(c * C, C), C)
            kt = (k[at, lanes].astype(F32) * tail[h, at, :]).T.astype(BF16)
            prevs[h, c] = s
            return last(h, c) * s + dot(kt, v[at, lanes], NN)

        edge_state[h] = lax.fori_loop(0, chunks, one, jnp.zeros((D, D), F32), unroll=True)
        return 0

    lax.fori_loop(0, heads, own_forward, 0, unroll=True)

    def stage_forward(j, _):
        at = pl.ds(pl.multiple_of(j * srow, srow), srow)
        fs[j] = edge_state[:, at, :].reshape(heads * srow, D).astype(BF16)
        return 0

    lax.fori_loop(0, segments, stage_forward, 0)
    exchange(fs, fr, fsem.at[0], fsem.at[1])

    loads[2].wait()
    loads[3].wait()

    def prepare(i, _):
        h, c = i // chunks, lax.rem(i, chunks)
        at = pl.ds(pl.multiple_of(c * C, C), C)
        lanes = pl.ds(pl.multiple_of(h * D, D), D)
        a = rate(h)
        n = ncol[at, :]
        nc = jnp.concatenate([n, n], axis=1)
        nr = nrow[c][0:1, :]
        gap = (
            lax.broadcasted_iota(jnp.int32, (C, C), 0) - lax.broadcasted_iota(jnp.int32, (C, C), 1)
        ).astype(F32)
        dn = nc - nr
        w[i] = jnp.where(gap >= 0, jnp.exp2(-a * gap - dn), 0.0)
        weight = jnp.where(gap <= 0, jnp.exp2(a * gap + dn), 0.0)
        wt[i] = weight
        qc = q[at, lanes]
        pk[i] = (dot(k[at, lanes], qc, NT) * weight).astype(BF16)
        qh[i] = (qc.astype(F32) * hin[h, at, :]).T.astype(BF16)
        return 0

    lax.fori_loop(0, heads * chunks, prepare, 0, unroll=True)

    def own_backward(h):
        lanes = pl.ds(h * D, D)
        col = g.at[:, lanes]
        pltpu.make_async_copy(col, col, gr.at[h]).wait()

        def one(i, s):
            c = chunks - 1 - i
            at = pl.ds(pl.multiple_of(c * C, C), C)
            nexts[h, c] = s
            return last(h, c) * s + dot(qh[h * chunks + c], g[at, lanes], NN)

        edge_state[h] = lax.fori_loop(0, chunks, one, jnp.zeros((D, D), F32), unroll=True)

    def send_backward(p):
        def stage(j, _):
            at = pl.ds(pl.multiple_of(j * srow, srow), srow)
            bs[p, j] = edge_state[pl.ds(2 * p, 2), at, :].reshape(2 * srow, D).astype(BF16)
            return 0

        lax.fori_loop(0, segments, stage, 0)
        exchange(bs.at[p], br.at[p], bsem.at[p, 0], bsem.at[p, 1])

    def scan_forward():
        arrived(fr, fsem.at[1])

        def one(d, s):
            fo[d] = s.astype(BF16)
            return seg_decay(0, heads, d) * s + fr[d].astype(F32)

        lax.fori_loop(0, segments, one, st[...].reshape(heads * srow, D), unroll=True)
        exchange(fo, fin, fsem.at[2], fsem.at[3])

    def scan_backward(p):
        arrived(br.at[p], bsem.at[p, 1])

        def one(i, s):
            d = segments - 1 - i
            bo[p, d] = s.astype(BF16)
            return seg_decay(2 * p, 2 * p + 2, d) * s + br[p, d].astype(F32)

        whole = lax.fori_loop(0, segments, one, jnp.zeros((2 * srow, D), F32), unroll=True)
        sg_ref[pl.ds(2 * p, 2)] = whole.reshape(2, srow, D)
        exchange(bo.at[p], bin_.at[p], bsem.at[p, 2], bsem.at[p, 3])

    def inside(h):
        lanes = pl.ds(h * D, D)

        def one(c, _):
            at = pl.ds(pl.multiple_of(c * C, C), C)
            i = h * chunks + c
            gc, vc = g[at, lanes], v[at, lanes]
            grad = (dot(gc, vc, NT) * w[i]).astype(BF16)
            dqi[at, lanes] = dot(grad, k[at, lanes], NN)
            turned = (dot(vc, gc, NT) * wt[i]).astype(BF16)
            dki[at, lanes] = dot(turned, q[at, lanes], NN)
            dvi[at, lanes] = dot(pk[i], gc, NN)
            return 0

        lax.fori_loop(0, chunks, one, 0, unroll=True)

    def finish_query():
        arrived(fin, fsem.at[3])
        got = fin[...].astype(F32)
        for h in range(heads):
            fins[h] = got[:, h * srow:(h + 1) * srow, :].reshape(D, D)

        def one(i, _):
            h, c = i // chunks, lax.rem(i, chunks)
            at = pl.ds(pl.multiple_of(c * C, C), C)
            lanes = pl.ds(pl.multiple_of(h * D, D), D)
            hits = count(start + c * C - 1) - count(start - 1)
            reach = row(-rate(h) * (c * C).astype(F32) - hits)
            state = (prevs[h, c] + reach * fins[h]).astype(BF16)
            dq_ref[at, lanes] = (dqi[at, lanes] + hin[h, at, :] * dot(g[at, lanes], state, NT)).astype(BF16)
            return 0

        lax.fori_loop(0, heads * chunks, one, 0, unroll=True)

    def finish_keys(p):
        arrived(bin_.at[p], bsem.at[p, 3])
        got = bin_[p].astype(F32)
        for e in range(2):
            bins[2 * p + e] = got[:, e * srow:(e + 1) * srow, :].reshape(D, D)

        def one(i, _):
            h, c = 2 * p + i // chunks, lax.rem(i, chunks)
            at = pl.ds(pl.multiple_of(c * C, C), C)
            lanes = pl.ds(pl.multiple_of(h * D, D), D)
            hits = count(start + tokens - 1) - count(start + c * C + C - 1)
            reach = row(-rate(h) * (tokens - C - c * C).astype(F32) - hits)
            grad = (nexts[h, c] + reach * bins[h]).astype(BF16)
            scale = tail[h, at, :]
            dk_ref[at, lanes] = (dki[at, lanes] + scale * dot(v[at, lanes], grad, NT)).astype(BF16)
            dv_ref[at, lanes] = (dvi[at, lanes] + scale * dot(k[at, lanes], grad, NN)).astype(BF16)
            return 0

        lax.fori_loop(0, 2 * chunks, one, 0, unroll=True)

    own_backward(0)
    own_backward(1)
    send_backward(0)
    scan_forward()
    inside(0)
    own_backward(2)
    own_backward(3)
    send_backward(1)
    scan_backward(0)
    inside(1)
    inside(2)
    scan_backward(1)
    inside(3)
    finish_query()
    finish_keys(0)
    finish_keys(1)

    sent = og_hbm.at[:, pl.ds(0, (groups - 1) * width)]
    pltpu.make_async_copy(sent, sent, gs).wait()
    arrived(fs, fsem.at[0])
    arrived(fo, fsem.at[2])
    for p in range(heads // 2):
        arrived(bs.at[p], bsem.at[p, 0])
        arrived(bo.at[p], bsem.at[p, 2])


def store(a, b, c, s, oa, ob, oc, os, sem):
    rows = a.shape[0] // 4
    copies = [pltpu.make_async_copy(s, os, sem.at[12])]
    for i in range(4):
        at = pl.ds(i * rows, rows)
        for j, (src, dst) in enumerate(((a, oa), (b, ob), (c, oc))):
            copies.append(pltpu.make_async_copy(src.at[at], dst.at[at], sem.at[3 * i + j]))
    for copy in copies:
        copy.start()
    for copy in copies:
        copy.wait()


def shards(queries, keys, values, out_grad, state_in, exponents, boundaries):
    tokens, width = queries.shape
    heads = width // D
    chunks = tokens // C
    segments = lax.axis_size("ctx")
    srow = D // segments
    total = tokens * segments
    sizes = (heads, chunks, tokens, segments, boundaries.shape[0], total)
    hbm = pl.BlockSpec(memory_space=pltpu.HBM)
    vmem = pl.BlockSpec(memory_space=pltpu.VMEM)
    smem = pl.BlockSpec(memory_space=pltpu.SMEM)
    n = heads * chunks
    slab = lambda rows: pltpu.VMEM((segments, rows, D), BF16)
    pair = lambda: pltpu.VMEM((heads // 2, segments, 2 * srow, D), BF16)
    results = pl.pallas_call(
        functools.partial(layer, sizes),
        name="layer",
        out_shape=(
            pltpu.VMEM((tokens, width), BF16),
            pltpu.VMEM((tokens, width), BF16),
            pltpu.VMEM((tokens, width), BF16),
            pltpu.VMEM((heads, srow, D), F32),
        ),
        in_specs=[hbm] * 5 + [smem] * 2,
        out_specs=(vmem,) * 4,
        scratch_shapes=[
            pltpu.VMEM((tokens, width), BF16),
            pltpu.VMEM((tokens, width), BF16),
            pltpu.VMEM((tokens, width), BF16),
            pltpu.VMEM((tokens, width), BF16),
            pltpu.VMEM((heads, srow, D), F32),
            pltpu.VMEM((tokens, D), F32),
            pltpu.VMEM((chunks, 8, C), F32),
            pltpu.VMEM((heads, tokens, D), F32),
            pltpu.VMEM((heads, tokens, D), F32),
            pltpu.VMEM((n, C, C), F32),
            pltpu.VMEM((n, C, C), F32),
            pltpu.VMEM((n, C, C), BF16),
            pltpu.VMEM((n, D, C), BF16),
            pltpu.VMEM((tokens, width), F32),
            pltpu.VMEM((tokens, width), F32),
            pltpu.VMEM((tokens, width), F32),
            pltpu.VMEM((heads, chunks, D, D), F32),
            pltpu.VMEM((heads, chunks, D, D), F32),
            pltpu.VMEM((heads, D, D), F32),
            slab(heads * srow),
            slab(heads * srow),
            slab(heads * srow),
            slab(heads * srow),
            pltpu.VMEM((heads, D, D), F32),
            pair(),
            pair(),
            pair(),
            pair(),
            pltpu.VMEM((heads, D, D), F32),
            pltpu.SemaphoreType.DMA((4,)),
            pltpu.SemaphoreType.DMA,
            pltpu.SemaphoreType.DMA((heads,)),
            pltpu.SemaphoreType.DMA((4,)),
            pltpu.SemaphoreType.DMA((heads // 2, 4)),
        ],
        compiler_params=pltpu.CompilerParams(
            collective_id=0, has_side_effects=True, vmem_limit_bytes=48 << 20
        ),
    )(*[
        pltpu.with_memory_space_constraint(a, pltpu.HBM)
        for a in (queries, keys, values, out_grad, state_in, exponents, boundaries)
    ])
    whole = jax.ShapeDtypeStruct((tokens, width), BF16)
    return pl.pallas_call(
        store,
        name="store",
        out_shape=(whole, whole, whole, jax.ShapeDtypeStruct((heads, srow, D), F32)),
        in_specs=[vmem] * 4,
        out_specs=(hbm,) * 4,
        scratch_shapes=[pltpu.SemaphoreType.DMA((13,))],
        compiler_params=pltpu.CompilerParams(vmem_limit_bytes=4 << 20),
    )(*results)


def solution(mesh):
    in_specs = (
        P("ctx", "head"),
        P("ctx", "head"),
        P("ctx", "head"),
        P(("ctx", "head"), None),
        P("head", None, None),
        P("head"),
        P(),
    )
    out_specs = (P("ctx", "head"), P("ctx", "head"), P("ctx", "head"), P("head", "ctx", None))
    return jax.shard_map(shards, mesh=mesh, in_specs=in_specs, out_specs=out_specs, check_vma=False)
```

```python
import functools

import jax
import jax.numpy as jnp
from jax import lax
from jax.experimental import pallas as pl
from jax.experimental.pallas import tpu as pltpu
from jax.sharding import PartitionSpec as P

D = 128
C = 256
MESH = pl.DeviceIdType.MESH
F32 = jnp.float32
BF16 = jnp.bfloat16
NN = ((1,), (0,))
NT = ((1,), (1,))


def dot(a, b, dims):
    return lax.dot_general(a, b, (dims, ((), ())), preferred_element_type=F32)


def far(step, size):
    return min(step, size - step)


def layer(
    sizes,
    q_hbm, k_hbm, v_hbm, og_hbm, st_hbm, exps, bnds,
    dq_ref, dk_ref, dv_ref, sg_ref, ki_ref, vi_ref, kl_ref, vl_ref, scale_ref, grad_ref,
    q, k, v, g, st, ncol, nrow, tail, hin, w, wt, pk, qh,
    dqi, dki, dvi, prevs, nexts, edge_state,
    fs, fr, fo, fin, fins, bs, br, bo, bin_, bins,
    cs, cr, co, ci, gs_out, gs_in,
    segd, lastd, befored, afterd,
    lsem, gs, gr, fsem, bsem, csem, osem, ssem,
):
    heads, chunks, tokens, segments, nbounds, total = sizes
    groups = 16
    ctx = lax.axis_index("ctx")
    me = lax.axis_index("head")
    z, core = ctx // 2, ctx % 2
    y, x = me // 4, me % 4
    rows_each = tokens // groups
    width = heads * D
    srow = D // segments
    zs = segments // 2

    head_steps = sorted(
        [(a, b) for a in range(4) for b in range(4) if a or b],
        key=lambda s: -(far(s[0], 4) + far(s[1], 4)),
    )
    ctx_steps = sorted(
        [(a, b) for a in range(segments // 2) for b in range(2) if a or b],
        key=lambda s: -far(s[0], segments // 2),
    )

    def head_peer(step):
        return lax.rem(y + step[0], 4) * 4 + lax.rem(x + step[1], 4)

    def ctx_peer(step):
        return lax.rem(z + step[0], segments // 2) * 2 + lax.rem(core + step[1], 2)

    barrier = pltpu.get_barrier_semaphore()
    for s in head_steps:
        pl.semaphore_signal(barrier, inc=1, device_id=(ctx, head_peer(s)), device_id_type=MESH)
    for s in ctx_steps:
        pl.semaphore_signal(barrier, inc=1, device_id=(ctx_peer(s), me), device_id_type=MESH)

    loads = [
        pltpu.make_async_copy(k_hbm, k, lsem.at[0]),
        pltpu.make_async_copy(v_hbm, v, lsem.at[1]),
        pltpu.make_async_copy(q_hbm, q, lsem.at[2]),
        pltpu.make_async_copy(st_hbm.at[:, pl.ds(pl.multiple_of(ctx * srow, srow), srow), :], st, lsem.at[3]),
    ]
    for c in loads:
        c.start()

    start = ctx * tokens

    def count(t):
        n = jnp.int32(0)
        for b in range(nbounds):
            n = n + jnp.where(bnds[b] <= t, 1, 0)
        return n.astype(F32)

    def rate(h):
        return exps[h].astype(F32) * (1.0 / (4.0 * total))

    def tile(value):
        return jnp.exp2(jnp.full((8, D), value, F32))

    def segment_decays(d, _):
        hits = count((d + 1) * tokens - 1) - count(d * tokens - 1)
        for h in range(heads):
            segd[h, d] = tile(-rate(h) * float(tokens) - hits)
        return 0

    def chunk_decays(c, _):
        low, high = count(start + c * C - 1), count(start + c * C + C - 1)
        first, end = count(start - 1), count(start + tokens - 1)
        passed = (c * C).astype(F32)
        for h in range(heads):
            lastd[h, c] = tile(-rate(h) * float(C) - (high - low))
            befored[h, c] = tile(-rate(h) * passed - (low - first))
            afterd[h, c] = tile(-rate(h) * (float(tokens - C) - passed) - (end - high))
        return 0

    def counts(c, _):
        first = start + c * C
        tc = first + lax.broadcasted_iota(jnp.int32, (C, D), 0)
        tr = first + lax.broadcasted_iota(jnp.int32, (8, C), 1)
        nc = jnp.zeros((C, D), F32)
        nr = jnp.zeros((8, C), F32)
        for b in range(nbounds):
            nc = nc + jnp.where(tc >= bnds[b], 1.0, 0.0)
            nr = nr + jnp.where(tr >= bnds[b], 1.0, 0.0)
        ncol[pl.ds(pl.multiple_of(c * C, C), C), :] = nc
        nrow[c] = nr
        return 0

    def rates(i, _):
        h, c = i // chunks, lax.rem(i, chunks)
        at = pl.ds(pl.multiple_of(c * C, C), C)
        a = rate(h)
        n = ncol[at, :]
        place = lax.broadcasted_iota(jnp.int32, (C, D), 0).astype(F32)
        before = count(start + c * C - 1)
        after = count(start + c * C + C - 1)
        hin[h, at, :] = jnp.exp2(-a * (place + 1.0) - (n - before))
        tail[h, at, :] = jnp.exp2(-a * ((C - 1.0) - place) - (after - n))
        return 0

    pl.semaphore_wait(barrier, len(head_steps) + len(ctx_steps))

    mine = pl.ds(pl.multiple_of(me * rows_each, rows_each), rows_each)
    def send_head(h, _):
        for s in head_steps:
            peer = head_peer(s)
            at = pl.multiple_of(peer * width + h * D, D)
            pltpu.make_async_remote_copy(
                src_ref=og_hbm.at[:, pl.ds(at, D)],
                dst_ref=g.at[mine, pl.ds(pl.multiple_of(h * D, D), D)],
                send_sem=gs,
                recv_sem=gr.at[h],
                device_id=(ctx, peer),
                device_id_type=MESH,
            ).start()
        return 0

    lax.fori_loop(0, heads, send_head, 0)
    for h in range(heads):
        at = pl.multiple_of(me * width + h * D, D)
        pltpu.make_async_copy(og_hbm.at[:, pl.ds(at, D)], g.at[mine, pl.ds(h * D, D)], gr.at[h]).start()

    lax.fori_loop(0, chunks, counts, 0)
    lax.fori_loop(0, heads * chunks, rates, 0)
    lax.fori_loop(0, chunks, chunk_decays, 0)
    lax.fori_loop(0, segments, segment_decays, 0)

    def exchange(src, dst, ssem, rsem):
        for s in ctx_steps:
            peer = ctx_peer(s)
            pltpu.make_async_remote_copy(
                src_ref=src.at[peer],
                dst_ref=dst.at[ctx],
                send_sem=ssem,
                recv_sem=rsem,
                device_id=(peer, me),
                device_id_type=MESH,
            ).start()
        dst[ctx] = src[ctx]

    def arrived(buf, sem):
        part = buf.at[pl.ds(0, segments - 1)]
        pltpu.make_async_copy(part, part, sem).wait()

    def seg_decay(lo, hi, d):
        return segd[lo:hi, d].reshape((hi - lo) * srow, D)

    def last(h, c):
        return lastd[h, c, 0:1, :]

    loads[0].wait()
    loads[1].wait()

    def own_forward(h, _):
        lanes = pl.ds(pl.multiple_of(h * D, D), D)

        def one(c, s):
            at = pl.ds(pl.multiple_of(c * C, C), C)
            kt = (k[at, lanes].astype(F32) * tail[h, at, :]).T.astype(BF16)
            prevs[h, c] = s
            return last(h, c) * s + dot(kt, v[at, lanes], NN)

        edge_state[h] = lax.fori_loop(0, chunks, one, jnp.zeros((D, D), F32), unroll=True)
        return 0

    lax.fori_loop(0, heads, own_forward, 0, unroll=True)

    def stage_forward(j, _):
        at = pl.ds(pl.multiple_of(j * srow, srow), srow)
        fs[j] = edge_state[:, at, :].reshape(heads * srow, D).astype(BF16)
        return 0

    lax.fori_loop(0, segments, stage_forward, 0)
    exchange(fs, fr, fsem.at[0], fsem.at[1])

    loads[2].wait()
    loads[3].wait()

    def prepare(i, _):
        h, c = i // chunks, lax.rem(i, chunks)
        at = pl.ds(pl.multiple_of(c * C, C), C)
        lanes = pl.ds(pl.multiple_of(h * D, D), D)
        a = rate(h)
        n = ncol[at, :]
        nc = jnp.concatenate([n, n], axis=1)
        nr = nrow[c][0:1, :]
        gap = (
            lax.broadcasted_iota(jnp.int32, (C, C), 0) - lax.broadcasted_iota(jnp.int32, (C, C), 1)
        ).astype(F32)
        dn = nc - nr
        w[i] = jnp.where(gap >= 0, jnp.exp2(-a * gap - dn), 0.0)
        weight = jnp.where(gap <= 0, jnp.exp2(a * gap + dn), 0.0)
        wt[i] = weight
        qc = q[at, lanes]
        pk[i] = (dot(k[at, lanes], qc, NT) * weight).astype(BF16)
        qh[i] = (qc.astype(F32) * hin[h, at, :]).T.astype(BF16)
        return 0

    lax.fori_loop(0, heads * chunks, prepare, 0, unroll=True)
    kl_ref[...] = k[:, (heads - 1) * D:]
    vl_ref[...] = v[:, (heads - 1) * D:]
    scale_ref[...] = tail[heads - 1]

    def own_backward(h):
        lanes = pl.ds(h * D, D)
        col = g.at[:, lanes]
        pltpu.make_async_copy(col, col, gr.at[h]).wait()

        def one(i, s):
            c = chunks - 1 - i
            at = pl.ds(pl.multiple_of(c * C, C), C)
            nexts[h, c] = s
            return last(h, c) * s + dot(qh[h * chunks + c], g[at, lanes], NN)

        edge_state[h] = lax.fori_loop(0, chunks, one, jnp.zeros((D, D), F32), unroll=True)

    def send_backward(p):
        def stage(j, _):
            at = pl.ds(pl.multiple_of(j * srow, srow), srow)
            bs[p, j] = edge_state[pl.ds(2 * p, 2), at, :].reshape(2 * srow, D).astype(BF16)
            return 0

        lax.fori_loop(0, segments, stage, 0)
        exchange(bs.at[p], br.at[p], bsem.at[p, 0], bsem.at[p, 1])

    def send_single(e):
        h = 2 + e
        cs[e] = edge_state[h].reshape(zs, D // zs, D).astype(BF16)

        def copy(to):
            return pltpu.make_async_remote_copy(
                src_ref=cs.at[e, to], dst_ref=cr.at[e, ctx], send_sem=csem.at[e, 0], recv_sem=csem.at[e, 1],
                device_id=(2 * to + e, me), device_id_type=MESH,
            )

        for step in sorted(range(1, zs), key=lambda n: -far(n, zs)):
            copy(lax.rem(z + step, zs)).start()

        @pl.when(core == e)
        def _():
            cr[e, ctx] = cs[e, z]

        @pl.when(core != e)
        def _():
            copy(z).start()

    def scan_single(e):
        h = 2 + e

        @pl.when(core == e)
        def _():
            arrived(cr.at[e], csem.at[e, 1])

            def one(i, s):
                d = segments - 1 - i
                co[d] = s.astype(BF16)
                return segd[h, d, 0:1, :] * s + cr[e, d].astype(F32)

            whole = lax.fori_loop(0, segments, one, jnp.zeros((D // zs, D), F32), unroll=True)
            for step in ctx_steps:
                peer = ctx_peer(step)
                pltpu.make_async_remote_copy(
                    src_ref=co.at[peer], dst_ref=ci.at[e, z], send_sem=osem.at[e, 0], recv_sem=osem.at[e, 1],
                    device_id=(peer, me), device_id_type=MESH,
                ).start()
            ci[e, z] = co[ctx]
            sg_ref[h] = whole[e * srow:(e + 1) * srow, :]
            gs_out[...] = whole[(1 - e) * srow:(2 - e) * srow, :]
            swap_rows().start()

    def swap_rows():
        return pltpu.make_async_remote_copy(
            src_ref=gs_out, dst_ref=gs_in, send_sem=ssem.at[0], recv_sem=ssem.at[1],
            device_id=(2 * z + 1 - core, me), device_id_type=MESH,
        )

    def slots(buf, n, sem):
        part = buf.at[pl.ds(0, n)]
        pltpu.make_async_copy(part, part, sem).wait()

    def join_single(e):
        @pl.when(core == e)
        def _():
            slots(ci.at[e], zs - 1, osem.at[e, 1])

        @pl.when(core != e)
        def _():
            slots(ci.at[e], zs, osem.at[e, 1])

        bins[2 + e] = ci[e].astype(F32).reshape(D, D)

    def end_single():
        swap_rows().wait()
        for e in range(2):
            @pl.when(core == e)
            def _():
                sg_ref[3 - e] = gs_in[...]
                slots(cs.at[e], zs - 1, csem.at[e, 0])
                slots(co, segments - 1, osem.at[e, 0])

            @pl.when(core != e)
            def _():
                slots(cs.at[e], zs, csem.at[e, 0])

    def scan_forward():
        arrived(fr, fsem.at[1])

        def one(d, s):
            fo[d] = s.astype(BF16)
            return seg_decay(0, heads, d) * s + fr[d].astype(F32)

        lax.fori_loop(0, segments, one, st[...].reshape(heads * srow, D), unroll=True)
        exchange(fo, fin, fsem.at[2], fsem.at[3])

    def scan_backward(p):
        arrived(br.at[p], bsem.at[p, 1])

        def one(i, s):
            d = segments - 1 - i
            bo[p, d] = s.astype(BF16)
            return seg_decay(2 * p, 2 * p + 2, d) * s + br[p, d].astype(F32)

        whole = lax.fori_loop(0, segments, one, jnp.zeros((2 * srow, D), F32), unroll=True)
        sg_ref[pl.ds(2 * p, 2)] = whole.reshape(2, srow, D)
        exchange(bo.at[p], bin_.at[p], bsem.at[p, 2], bsem.at[p, 3])

    def inside(h):
        lanes = pl.ds(h * D, D)

        def one(c, _):
            at = pl.ds(pl.multiple_of(c * C, C), C)
            i = h * chunks + c
            gc, vc = g[at, lanes], v[at, lanes]
            grad = (dot(gc, vc, NT) * w[i]).astype(BF16)
            dqi[at, lanes] = dot(grad, k[at, lanes], NN)
            turned = (dot(vc, gc, NT) * wt[i]).astype(BF16)
            dk_part, dv_part = dot(turned, q[at, lanes], NN), dot(pk[i], gc, NN)
            if h == heads - 1:
                ki_ref[at, :] = dk_part
                vi_ref[at, :] = dv_part
            else:
                dki[at, lanes] = dk_part
                dvi[at, lanes] = dv_part
            return 0

        lax.fori_loop(0, chunks, one, 0, unroll=True)

    def finish_query():
        arrived(fin, fsem.at[3])
        got = fin[...].astype(F32)
        for h in range(heads):
            fins[h] = got[:, h * srow:(h + 1) * srow, :].reshape(D, D)

        def one(i, _):
            h, c = i // chunks, lax.rem(i, chunks)
            at = pl.ds(pl.multiple_of(c * C, C), C)
            lanes = pl.ds(pl.multiple_of(h * D, D), D)
            state = (prevs[h, c] + befored[h, c, 0:1, :] * fins[h]).astype(BF16)
            dq_ref[at, lanes] = (dqi[at, lanes] + hin[h, at, :] * dot(g[at, lanes], state, NT)).astype(BF16)
            return 0

        lax.fori_loop(0, heads * chunks, one, 0, unroll=True)

    def join_pair(p):
        arrived(bin_.at[p], bsem.at[p, 3])
        got = bin_[p].astype(F32)
        for e in range(2):
            bins[2 * p + e] = got[:, e * srow:(e + 1) * srow, :].reshape(D, D)

    def finish_keys(h):
        lanes = pl.ds(h * D, D)

        def one(c, _):
            at = pl.ds(pl.multiple_of(c * C, C), C)
            grad = (nexts[h, c] + afterd[h, c, 0:1, :] * bins[h]).astype(BF16)
            scale = tail[h, at, :]
            dk_ref[at, lanes] = (dki[at, lanes] + scale * dot(v[at, lanes], grad, NT)).astype(BF16)
            dv_ref[at, lanes] = (dvi[at, lanes] + scale * dot(k[at, lanes], grad, NN)).astype(BF16)
            return 0

        lax.fori_loop(0, chunks, one, 0, unroll=True)

    own_backward(0)
    inside(0)
    own_backward(1)
    send_backward(0)
    scan_forward()
    inside(1)
    own_backward(2)
    send_single(0)
    scan_backward(0)
    own_backward(3)
    send_single(1)
    inside(2)
    scan_single(0)
    inside(3)
    scan_single(1)
    finish_query()
    join_pair(0)
    finish_keys(0)
    finish_keys(1)
    join_single(0)
    finish_keys(2)
    join_single(1)
    for c in range(chunks):
        grad_ref[c] = (nexts[heads - 1, c] + afterd[heads - 1, c, 0:1, :] * bins[heads - 1]).astype(BF16)

    sent = og_hbm.at[:, pl.ds(0, (groups - 1) * width)]
    pltpu.make_async_copy(sent, sent, gs).wait()
    arrived(fs, fsem.at[0])
    arrived(fo, fsem.at[2])
    arrived(bs.at[0], bsem.at[0, 0])
    arrived(bo.at[0], bsem.at[0, 2])
    end_single()


def store(dq, dk, dv, sg, ki, vi, kl, vl, scale, grad, dq_hbm, dk_hbm, dv_hbm, sg_hbm, lk, lv, sem):
    rows = dq.shape[0] // 4
    done = dk.shape[1] - D
    copies = [pltpu.make_async_copy(dq, dq_hbm, sem.at[0]), pltpu.make_async_copy(sg, sg_hbm, sem.at[1])]
    for j, (src, dst) in enumerate(((dk, dk_hbm), (dv, dv_hbm))):
        first = pl.ds(0, done)
        copies.append(pltpu.make_async_copy(src.at[:, first], dst.at[:, first], sem.at[2 + j]))
    for copy in copies:
        copy.start()
    for c in range(4):
        at = pl.ds(c * rows, rows)
        for j, (part, other, dims, last, dst) in enumerate(
            ((ki, vl, NT, lk, dk_hbm), (vi, kl, NN, lv, dv_hbm))
        ):
            last[at, :] = (part[at, :] + scale[at, :] * dot(other[at, :], grad[c], dims)).astype(BF16)
            copy = pltpu.make_async_copy(last.at[at], dst.at[at, pl.ds(done, D)], sem.at[4 + 2 * c + j])
            copy.start()
            copies.append(copy)
    for copy in copies:
        copy.wait()


def shards(queries, keys, values, out_grad, state_in, exponents, boundaries):
    tokens, width = queries.shape
    heads = width // D
    chunks = tokens // C
    segments = lax.axis_size("ctx")
    srow = D // segments
    total = tokens * segments
    sizes = (heads, chunks, tokens, segments, boundaries.shape[0], total)
    hbm = pl.BlockSpec(memory_space=pltpu.HBM)
    vmem = pl.BlockSpec(memory_space=pltpu.VMEM)
    smem = pl.BlockSpec(memory_space=pltpu.SMEM)
    n = heads * chunks
    slab = lambda rows: pltpu.VMEM((segments, rows, D), BF16)
    pair = lambda: pltpu.VMEM((1, segments, 2 * srow, D), BF16)
    results = pl.pallas_call(
        functools.partial(layer, sizes),
        name="layer",
        out_shape=(
            pltpu.VMEM((tokens, width), BF16),
            pltpu.VMEM((tokens, width), BF16),
            pltpu.VMEM((tokens, width), BF16),
            pltpu.VMEM((heads, srow, D), F32),
            pltpu.VMEM((tokens, D), F32),
            pltpu.VMEM((tokens, D), F32),
            pltpu.VMEM((tokens, D), BF16),
            pltpu.VMEM((tokens, D), BF16),
            pltpu.VMEM((tokens, D), F32),
            pltpu.VMEM((chunks, D, D), BF16),
        ),
        in_specs=[hbm] * 5 + [smem] * 2,
        out_specs=(vmem,) * 10,
        scratch_shapes=[
            pltpu.VMEM((tokens, width), BF16),
            pltpu.VMEM((tokens, width), BF16),
            pltpu.VMEM((tokens, width), BF16),
            pltpu.VMEM((tokens, width), BF16),
            pltpu.VMEM((heads, srow, D), F32),
            pltpu.VMEM((tokens, D), F32),
            pltpu.VMEM((chunks, 8, C), F32),
            pltpu.VMEM((heads, tokens, D), F32),
            pltpu.VMEM((heads, tokens, D), F32),
            pltpu.VMEM((n, C, C), F32),
            pltpu.VMEM((n, C, C), F32),
            pltpu.VMEM((n, C, C), BF16),
            pltpu.VMEM((n, D, C), BF16),
            pltpu.VMEM((tokens, width), F32),
            pltpu.VMEM((tokens, width), F32),
            pltpu.VMEM((tokens, width), F32),
            pltpu.VMEM((heads, chunks, D, D), F32),
            pltpu.VMEM((heads, chunks, D, D), F32),
            pltpu.VMEM((heads, D, D), F32),
            slab(heads * srow),
            slab(heads * srow),
            slab(heads * srow),
            slab(heads * srow),
            pltpu.VMEM((heads, D, D), F32),
            pair(),
            pair(),
            pair(),
            pair(),
            pltpu.VMEM((heads, D, D), F32),
            pltpu.VMEM((2, segments // 2, 2 * srow, D), BF16),
            pltpu.VMEM((2, segments, 2 * srow, D), BF16),
            pltpu.VMEM((segments, 2 * srow, D), BF16),
            pltpu.VMEM((2, segments // 2, 2 * srow, D), BF16),
            pltpu.VMEM((srow, D), F32),
            pltpu.VMEM((srow, D), F32),
            pltpu.VMEM((heads, segments, 8, D), F32),
            pltpu.VMEM((heads, chunks, 8, D), F32),
            pltpu.VMEM((heads, chunks, 8, D), F32),
            pltpu.VMEM((heads, chunks, 8, D), F32),
            pltpu.SemaphoreType.DMA((4,)),
            pltpu.SemaphoreType.DMA,
            pltpu.SemaphoreType.DMA((heads,)),
            pltpu.SemaphoreType.DMA((4,)),
            pltpu.SemaphoreType.DMA((1, 4)),
            pltpu.SemaphoreType.DMA((2, 2)),
            pltpu.SemaphoreType.DMA((2, 2)),
            pltpu.SemaphoreType.DMA((2,)),
        ],
        compiler_params=pltpu.CompilerParams(
            collective_id=0, has_side_effects=True, vmem_limit_bytes=48 << 20
        ),
    )(*[
        pltpu.with_memory_space_constraint(a, pltpu.HBM)
        for a in (queries, keys, values, out_grad, state_in, exponents, boundaries)
    ])
    whole = jax.ShapeDtypeStruct((tokens, width), BF16)
    return pl.pallas_call(
        store,
        name="store",
        out_shape=(whole, whole, whole, jax.ShapeDtypeStruct((heads, srow, D), F32)),
        in_specs=[vmem] * 10,
        out_specs=(hbm,) * 4,
        scratch_shapes=[
            pltpu.VMEM((tokens, D), BF16),
            pltpu.VMEM((tokens, D), BF16),
            pltpu.SemaphoreType.DMA((12,)),
        ],
        compiler_params=pltpu.CompilerParams(vmem_limit_bytes=4 << 20),
    )(*results)


def solution(mesh):
    in_specs = (
        P("ctx", "head"),
        P("ctx", "head"),
        P("ctx", "head"),
        P(("ctx", "head"), None),
        P("head", None, None),
        P("head"),
        P(),
    )
    out_specs = (P("ctx", "head"), P("ctx", "head"), P("ctx", "head"), P("head", "ctx", None))
    return jax.shard_map(shards, mesh=mesh, in_specs=in_specs, out_specs=out_specs, check_vma=False)
```

```python
import functools

import jax
import jax.numpy as jnp
from jax import lax
from jax.experimental import pallas as pl
from jax.experimental.pallas import tpu as pltpu
from jax.sharding import PartitionSpec as P

D = 128
C = 256
MESH = pl.DeviceIdType.MESH
F32 = jnp.float32
BF16 = jnp.bfloat16
NN = ((1,), (0,))
NT = ((1,), (1,))


def dot(a, b, dims):
    return lax.dot_general(a, b, (dims, ((), ())), preferred_element_type=F32)


def far(step, size):
    return min(step, size - step)


def layer(
    sizes,
    q_hbm, k_hbm, v_hbm, og_hbm, st_hbm, exps_hbm, bnds_hbm,
    dq_ref, dk_ref, dv_ref, sg_ref, ki_ref, vi_ref, kl_ref, vl_ref, scale_ref, grad_ref,
    exps, bnds, q, k, v, g, st, ncol, nrow, tail, hin, w, wt, pk, qh,
    dqi, dki, dvi, prevs, nexts, edge_state,
    fs, fr, fo, fin, fins, bs, br, bo, bin_, bins,
    cs, cr, co, ci, gs_out, gs_in,
    segd, lastd, befored, afterd,
    lsem, gs, gr, fsem, bsem, csem, osem, ssem,
):
    heads, chunks, tokens, segments, nbounds, total = sizes
    groups = 16
    ctx = lax.axis_index("ctx")
    me = lax.axis_index("head")
    z, core = ctx // 2, ctx % 2
    y, x = me // 4, me % 4
    rows_each = tokens // groups
    width = heads * D
    srow = D // segments
    zs = segments // 2

    head_steps = sorted(
        [(a, b) for a in range(4) for b in range(4) if a or b],
        key=lambda s: -(far(s[0], 4) + far(s[1], 4)),
    )
    ctx_steps = sorted(
        [(a, b) for a in range(segments // 2) for b in range(2) if a or b],
        key=lambda s: -far(s[0], segments // 2),
    )

    def head_peer(step):
        return lax.rem(y + step[0], 4) * 4 + lax.rem(x + step[1], 4)

    def ctx_peer(step):
        return lax.rem(z + step[0], segments // 2) * 2 + lax.rem(core + step[1], 2)

    barrier = pltpu.get_barrier_semaphore()
    for s in ctx_steps:
        pl.semaphore_signal(barrier, inc=1, device_id=(ctx_peer(s), me), device_id_type=MESH)
    for s in head_steps:
        pl.semaphore_signal(barrier, inc=1, device_id=(ctx, head_peer(s)), device_id_type=MESH)

    loads = [
        pltpu.make_async_copy(k_hbm, k, lsem.at[0]),
        pltpu.make_async_copy(v_hbm, v, lsem.at[1]),
        pltpu.make_async_copy(q_hbm, q, lsem.at[2]),
        pltpu.make_async_copy(st_hbm.at[:, pl.ds(pl.multiple_of(ctx * srow, srow), srow), :], st, lsem.at[3]),
    ]
    smalls = [
        pltpu.make_async_copy(exps_hbm, exps, lsem.at[4]),
        pltpu.make_async_copy(bnds_hbm, bnds, lsem.at[5]),
    ]
    for c in smalls + loads:
        c.start()

    start = ctx * tokens

    def count(t):
        n = jnp.int32(0)
        for b in range(nbounds):
            n = n + jnp.where(bnds[b] <= t, 1, 0)
        return n.astype(F32)

    def rate(h):
        return exps[h].astype(F32) * (1.0 / (4.0 * total))

    def tile(value):
        return jnp.exp2(jnp.full((8, D), value, F32))

    def segment_decays(d, _):
        hits = count((d + 1) * tokens - 1) - count(d * tokens - 1)
        for h in range(heads):
            segd[h, d] = tile(-rate(h) * float(tokens) - hits)
        return 0

    def chunk_decays(c, _):
        low, high = count(start + c * C - 1), count(start + c * C + C - 1)
        first, end = count(start - 1), count(start + tokens - 1)
        passed = (c * C).astype(F32)
        for h in range(heads):
            lastd[h, c] = tile(-rate(h) * float(C) - (high - low))
            befored[h, c] = tile(-rate(h) * passed - (low - first))
            afterd[h, c] = tile(-rate(h) * (float(tokens - C) - passed) - (end - high))
        return 0

    def counts(c, _):
        first = start + c * C
        tc = first + lax.broadcasted_iota(jnp.int32, (C, D), 0)
        tr = first + lax.broadcasted_iota(jnp.int32, (8, C), 1)
        nc = jnp.zeros((C, D), F32)
        nr = jnp.zeros((8, C), F32)
        for b in range(nbounds):
            nc = nc + jnp.where(tc >= bnds[b], 1.0, 0.0)
            nr = nr + jnp.where(tr >= bnds[b], 1.0, 0.0)
        ncol[pl.ds(pl.multiple_of(c * C, C), C), :] = nc
        nrow[c] = nr
        return 0

    def rates(i, _):
        h, c = i // chunks, lax.rem(i, chunks)
        at = pl.ds(pl.multiple_of(c * C, C), C)
        a = rate(h)
        n = ncol[at, :]
        place = lax.broadcasted_iota(jnp.int32, (C, D), 0).astype(F32)
        before = count(start + c * C - 1)
        after = count(start + c * C + C - 1)
        hin[h, at, :] = jnp.exp2(-a * (place + 1.0) - (n - before))
        tail[h, at, :] = jnp.exp2(-a * ((C - 1.0) - place) - (after - n))
        return 0

    pl.semaphore_wait(barrier, len(head_steps) + len(ctx_steps))

    mine = pl.ds(pl.multiple_of(me * rows_each, rows_each), rows_each)
    def send_head(h, _):
        for s in head_steps:
            peer = head_peer(s)
            at = pl.multiple_of(peer * width + h * D, D)
            pltpu.make_async_remote_copy(
                src_ref=og_hbm.at[:, pl.ds(at, D)],
                dst_ref=g.at[mine, pl.ds(pl.multiple_of(h * D, D), D)],
                send_sem=gs,
                recv_sem=gr.at[h],
                device_id=(ctx, peer),
                device_id_type=MESH,
            ).start()
        return 0

    lax.fori_loop(0, heads, send_head, 0)
    for h in range(heads):
        at = pl.multiple_of(me * width + h * D, D)
        pltpu.make_async_copy(og_hbm.at[:, pl.ds(at, D)], g.at[mine, pl.ds(h * D, D)], gr.at[h]).start()

    for c in smalls:
        c.wait()
    lax.fori_loop(0, chunks, counts, 0)
    lax.fori_loop(0, heads * chunks, rates, 0)
    lax.fori_loop(0, chunks, chunk_decays, 0)
    lax.fori_loop(0, segments, segment_decays, 0)

    def exchange(src, dst, ssem, rsem):
        for s in ctx_steps:
            peer = ctx_peer(s)
            pltpu.make_async_remote_copy(
                src_ref=src.at[peer],
                dst_ref=dst.at[ctx],
                send_sem=ssem,
                recv_sem=rsem,
                device_id=(peer, me),
                device_id_type=MESH,
            ).start()
        dst[ctx] = src[ctx]

    def arrived(buf, sem):
        part = buf.at[pl.ds(0, segments - 1)]
        pltpu.make_async_copy(part, part, sem).wait()

    def seg_decay(lo, hi, d):
        return segd[lo:hi, d].reshape((hi - lo) * srow, D)

    def last(h, c):
        return lastd[h, c, 0:1, :]

    loads[0].wait()
    loads[1].wait()

    def own_forward(h, _):
        lanes = pl.ds(pl.multiple_of(h * D, D), D)

        def one(c, s):
            at = pl.ds(pl.multiple_of(c * C, C), C)
            kt = (k[at, lanes].astype(F32) * tail[h, at, :]).T.astype(BF16)
            prevs[h, c] = s
            return last(h, c) * s + dot(kt, v[at, lanes], NN)

        edge_state[h] = lax.fori_loop(0, chunks, one, jnp.zeros((D, D), F32), unroll=True)
        return 0

    lax.fori_loop(0, heads, own_forward, 0, unroll=True)

    def stage_forward(j, _):
        at = pl.ds(pl.multiple_of(j * srow, srow), srow)
        fs[j] = edge_state[:, at, :].reshape(heads * srow, D).astype(BF16)
        return 0

    lax.fori_loop(0, segments, stage_forward, 0)
    exchange(fs, fr, fsem.at[0], fsem.at[1])

    loads[2].wait()
    loads[3].wait()

    def prepare(i, _):
        h, c = i // chunks, lax.rem(i, chunks)
        at = pl.ds(pl.multiple_of(c * C, C), C)
        lanes = pl.ds(pl.multiple_of(h * D, D), D)
        a = rate(h)
        n = ncol[at, :]
        nc = jnp.concatenate([n, n], axis=1)
        nr = nrow[c][0:1, :]
        gap = (
            lax.broadcasted_iota(jnp.int32, (C, C), 0) - lax.broadcasted_iota(jnp.int32, (C, C), 1)
        ).astype(F32)
        dn = nc - nr
        w[i] = jnp.where(gap >= 0, jnp.exp2(-a * gap - dn), 0.0)
        weight = jnp.where(gap <= 0, jnp.exp2(a * gap + dn), 0.0)
        wt[i] = weight
        qc = q[at, lanes]
        pk[i] = (dot(k[at, lanes], qc, NT) * weight).astype(BF16)
        qh[i] = (qc.astype(F32) * hin[h, at, :]).T.astype(BF16)
        return 0

    lax.fori_loop(0, heads * chunks, prepare, 0, unroll=True)
    kl_ref[...] = k[:, (heads - 1) * D:]
    vl_ref[...] = v[:, (heads - 1) * D:]
    scale_ref[...] = tail[heads - 1]

    def own_backward(h):
        lanes = pl.ds(h * D, D)
        col = g.at[:, lanes]
        pltpu.make_async_copy(col, col, gr.at[h]).wait()

        def one(i, s):
            c = chunks - 1 - i
            at = pl.ds(pl.multiple_of(c * C, C), C)
            nexts[h, c] = s
            return last(h, c) * s + dot(qh[h * chunks + c], g[at, lanes], NN)

        edge_state[h] = lax.fori_loop(0, chunks, one, jnp.zeros((D, D), F32), unroll=True)

    def send_backward(p):
        def stage(j, _):
            at = pl.ds(pl.multiple_of(j * srow, srow), srow)
            bs[p, j] = edge_state[pl.ds(2 * p, 2), at, :].reshape(2 * srow, D).astype(BF16)
            return 0

        lax.fori_loop(0, segments, stage, 0)
        exchange(bs.at[p], br.at[p], bsem.at[p, 0], bsem.at[p, 1])

    def send_single(e):
        h = 2 + e
        cs[e] = edge_state[h].reshape(zs, D // zs, D).astype(BF16)

        def copy(to):
            return pltpu.make_async_remote_copy(
                src_ref=cs.at[e, to], dst_ref=cr.at[e, ctx], send_sem=csem.at[e, 0], recv_sem=csem.at[e, 1],
                device_id=(2 * to + e, me), device_id_type=MESH,
            )

        for step in sorted(range(1, zs), key=lambda n: -far(n, zs)):
            copy(lax.rem(z + step, zs)).start()

        @pl.when(core == e)
        def _():
            cr[e, ctx] = cs[e, z]

        @pl.when(core != e)
        def _():
            copy(z).start()

    def scan_single(e):
        h = 2 + e

        @pl.when(core == e)
        def _():
            arrived(cr.at[e], csem.at[e, 1])

            def one(i, s):
                d = segments - 1 - i
                co[d] = s.astype(BF16)
                return segd[h, d, 0:1, :] * s + cr[e, d].astype(F32)

            whole = lax.fori_loop(0, segments, one, jnp.zeros((D // zs, D), F32), unroll=True)
            for step in ctx_steps:
                peer = ctx_peer(step)
                pltpu.make_async_remote_copy(
                    src_ref=co.at[peer], dst_ref=ci.at[e, z], send_sem=osem.at[e, 0], recv_sem=osem.at[e, 1],
                    device_id=(peer, me), device_id_type=MESH,
                ).start()
            ci[e, z] = co[ctx]
            sg_ref[h] = whole[e * srow:(e + 1) * srow, :]
            gs_out[...] = whole[(1 - e) * srow:(2 - e) * srow, :]
            swap_rows().start()

    def swap_rows():
        return pltpu.make_async_remote_copy(
            src_ref=gs_out, dst_ref=gs_in, send_sem=ssem.at[0], recv_sem=ssem.at[1],
            device_id=(2 * z + 1 - core, me), device_id_type=MESH,
        )

    def slots(buf, n, sem):
        part = buf.at[pl.ds(0, n)]
        pltpu.make_async_copy(part, part, sem).wait()

    def join_single(e):
        @pl.when(core == e)
        def _():
            slots(ci.at[e], zs - 1, osem.at[e, 1])

        @pl.when(core != e)
        def _():
            slots(ci.at[e], zs, osem.at[e, 1])

        bins[2 + e] = ci[e].astype(F32).reshape(D, D)

    def end_single():
        swap_rows().wait()
        for e in range(2):
            @pl.when(core == e)
            def _():
                sg_ref[3 - e] = gs_in[...]
                slots(cs.at[e], zs - 1, csem.at[e, 0])
                slots(co, segments - 1, osem.at[e, 0])

            @pl.when(core != e)
            def _():
                slots(cs.at[e], zs, csem.at[e, 0])

    def scan_forward():
        arrived(fr, fsem.at[1])

        def one(d, s):
            fo[d] = s.astype(BF16)
            return seg_decay(0, heads, d) * s + fr[d].astype(F32)

        lax.fori_loop(0, segments, one, st[...].reshape(heads * srow, D), unroll=True)
        exchange(fo, fin, fsem.at[2], fsem.at[3])

    def scan_backward(p):
        arrived(br.at[p], bsem.at[p, 1])

        def one(i, s):
            d = segments - 1 - i
            bo[p, d] = s.astype(BF16)
            return seg_decay(2 * p, 2 * p + 2, d) * s + br[p, d].astype(F32)

        whole = lax.fori_loop(0, segments, one, jnp.zeros((2 * srow, D), F32), unroll=True)
        sg_ref[pl.ds(2 * p, 2)] = whole.reshape(2, srow, D)
        exchange(bo.at[p], bin_.at[p], bsem.at[p, 2], bsem.at[p, 3])

    def inside(h):
        lanes = pl.ds(h * D, D)

        def one(c, _):
            at = pl.ds(pl.multiple_of(c * C, C), C)
            i = h * chunks + c
            gc, vc = g[at, lanes], v[at, lanes]
            grad = (dot(gc, vc, NT) * w[i]).astype(BF16)
            dqi[at, lanes] = dot(grad, k[at, lanes], NN)
            turned = (dot(vc, gc, NT) * wt[i]).astype(BF16)
            dk_part, dv_part = dot(turned, q[at, lanes], NN), dot(pk[i], gc, NN)
            if h == heads - 1:
                ki_ref[at, :] = dk_part
                vi_ref[at, :] = dv_part
            else:
                dki[at, lanes] = dk_part
                dvi[at, lanes] = dv_part
            return 0

        lax.fori_loop(0, chunks, one, 0, unroll=True)

    def finish_query():
        arrived(fin, fsem.at[3])
        got = fin[...].astype(F32)
        for h in range(heads):
            fins[h] = got[:, h * srow:(h + 1) * srow, :].reshape(D, D)

        def one(i, _):
            h, c = i // chunks, lax.rem(i, chunks)
            at = pl.ds(pl.multiple_of(c * C, C), C)
            lanes = pl.ds(pl.multiple_of(h * D, D), D)
            state = (prevs[h, c] + befored[h, c, 0:1, :] * fins[h]).astype(BF16)
            dq_ref[at, lanes] = (dqi[at, lanes] + hin[h, at, :] * dot(g[at, lanes], state, NT)).astype(BF16)
            return 0

        lax.fori_loop(0, heads * chunks, one, 0, unroll=True)

    def join_pair(p):
        arrived(bin_.at[p], bsem.at[p, 3])
        got = bin_[p].astype(F32)
        for e in range(2):
            bins[2 * p + e] = got[:, e * srow:(e + 1) * srow, :].reshape(D, D)

    def finish_keys(h):
        lanes = pl.ds(h * D, D)

        def one(c, _):
            at = pl.ds(pl.multiple_of(c * C, C), C)
            grad = (nexts[h, c] + afterd[h, c, 0:1, :] * bins[h]).astype(BF16)
            scale = tail[h, at, :]
            dk_ref[at, lanes] = (dki[at, lanes] + scale * dot(v[at, lanes], grad, NT)).astype(BF16)
            dv_ref[at, lanes] = (dvi[at, lanes] + scale * dot(k[at, lanes], grad, NN)).astype(BF16)
            return 0

        lax.fori_loop(0, chunks, one, 0, unroll=True)

    own_backward(0)
    inside(0)
    own_backward(1)
    send_backward(0)
    scan_forward()
    inside(1)
    own_backward(2)
    send_single(0)
    scan_backward(0)
    own_backward(3)
    send_single(1)
    scan_single(0)
    inside(2)
    inside(3)
    scan_single(1)
    finish_query()
    join_pair(0)
    finish_keys(0)
    finish_keys(1)
    join_single(0)
    finish_keys(2)
    join_single(1)
    for c in range(chunks):
        grad_ref[c] = (nexts[heads - 1, c] + afterd[heads - 1, c, 0:1, :] * bins[heads - 1]).astype(BF16)

    sent = og_hbm.at[:, pl.ds(0, (groups - 1) * width)]
    pltpu.make_async_copy(sent, sent, gs).wait()
    arrived(fs, fsem.at[0])
    arrived(fo, fsem.at[2])
    arrived(bs.at[0], bsem.at[0, 0])
    arrived(bo.at[0], bsem.at[0, 2])
    end_single()


def store(dq, dk, dv, sg, ki, vi, kl, vl, scale, grad, dq_hbm, dk_hbm, dv_hbm, sg_hbm, lk, lv, sem):
    rows = dq.shape[0] // 4
    done = dk.shape[1] - D
    copies = [pltpu.make_async_copy(dq, dq_hbm, sem.at[0]), pltpu.make_async_copy(sg, sg_hbm, sem.at[1])]
    for j, (src, dst) in enumerate(((dk, dk_hbm), (dv, dv_hbm))):
        first = pl.ds(0, done)
        copies.append(pltpu.make_async_copy(src.at[:, first], dst.at[:, first], sem.at[2 + j]))
    for copy in copies:
        copy.start()
    for c in range(4):
        at = pl.ds(c * rows, rows)
        for j, (part, other, dims, last, dst) in enumerate(
            ((ki, vl, NT, lk, dk_hbm), (vi, kl, NN, lv, dv_hbm))
        ):
            last[at, :] = (part[at, :] + scale[at, :] * dot(other[at, :], grad[c], dims)).astype(BF16)
            copy = pltpu.make_async_copy(last.at[at], dst.at[at, pl.ds(done, D)], sem.at[4 + 2 * c + j])
            copy.start()
            copies.append(copy)
    for copy in copies:
        copy.wait()


def shards(queries, keys, values, out_grad, state_in, exponents, boundaries):
    tokens, width = queries.shape
    heads = width // D
    chunks = tokens // C
    segments = lax.axis_size("ctx")
    srow = D // segments
    total = tokens * segments
    sizes = (heads, chunks, tokens, segments, boundaries.shape[0], total)
    hbm = pl.BlockSpec(memory_space=pltpu.HBM)
    vmem = pl.BlockSpec(memory_space=pltpu.VMEM)
    n = heads * chunks
    slab = lambda rows: pltpu.VMEM((segments, rows, D), BF16)
    pair = lambda: pltpu.VMEM((1, segments, 2 * srow, D), BF16)
    results = pl.pallas_call(
        functools.partial(layer, sizes),
        name="layer",
        out_shape=(
            pltpu.VMEM((tokens, width), BF16),
            pltpu.VMEM((tokens, width), BF16),
            pltpu.VMEM((tokens, width), BF16),
            pltpu.VMEM((heads, srow, D), F32),
            pltpu.VMEM((tokens, D), F32),
            pltpu.VMEM((tokens, D), F32),
            pltpu.VMEM((tokens, D), BF16),
            pltpu.VMEM((tokens, D), BF16),
            pltpu.VMEM((tokens, D), F32),
            pltpu.VMEM((chunks, D, D), BF16),
        ),
        in_specs=[hbm] * 7,
        out_specs=(vmem,) * 10,
        scratch_shapes=[
            pltpu.SMEM((heads,), jnp.int32),
            pltpu.SMEM((boundaries.shape[0],), jnp.int32),
            pltpu.VMEM((tokens, width), BF16),
            pltpu.VMEM((tokens, width), BF16),
            pltpu.VMEM((tokens, width), BF16),
            pltpu.VMEM((tokens, width), BF16),
            pltpu.VMEM((heads, srow, D), F32),
            pltpu.VMEM((tokens, D), F32),
            pltpu.VMEM((chunks, 8, C), F32),
            pltpu.VMEM((heads, tokens, D), F32),
            pltpu.VMEM((heads, tokens, D), F32),
            pltpu.VMEM((n, C, C), F32),
            pltpu.VMEM((n, C, C), F32),
            pltpu.VMEM((n, C, C), BF16),
            pltpu.VMEM((n, D, C), BF16),
            pltpu.VMEM((tokens, width), F32),
            pltpu.VMEM((tokens, width), F32),
            pltpu.VMEM((tokens, width), F32),
            pltpu.VMEM((heads, chunks, D, D), F32),
            pltpu.VMEM((heads, chunks, D, D), F32),
            pltpu.VMEM((heads, D, D), F32),
            slab(heads * srow),
            slab(heads * srow),
            slab(heads * srow),
            slab(heads * srow),
            pltpu.VMEM((heads, D, D), F32),
            pair(),
            pair(),
            pair(),
            pair(),
            pltpu.VMEM((heads, D, D), F32),
            pltpu.VMEM((2, segments // 2, 2 * srow, D), BF16),
            pltpu.VMEM((2, segments, 2 * srow, D), BF16),
            pltpu.VMEM((segments, 2 * srow, D), BF16),
            pltpu.VMEM((2, segments // 2, 2 * srow, D), BF16),
            pltpu.VMEM((srow, D), F32),
            pltpu.VMEM((srow, D), F32),
            pltpu.VMEM((heads, segments, 8, D), F32),
            pltpu.VMEM((heads, chunks, 8, D), F32),
            pltpu.VMEM((heads, chunks, 8, D), F32),
            pltpu.VMEM((heads, chunks, 8, D), F32),
            pltpu.SemaphoreType.DMA((6,)),
            pltpu.SemaphoreType.DMA,
            pltpu.SemaphoreType.DMA((heads,)),
            pltpu.SemaphoreType.DMA((4,)),
            pltpu.SemaphoreType.DMA((1, 4)),
            pltpu.SemaphoreType.DMA((2, 2)),
            pltpu.SemaphoreType.DMA((2, 2)),
            pltpu.SemaphoreType.DMA((2,)),
        ],
        compiler_params=pltpu.CompilerParams(
            collective_id=0, has_side_effects=True, vmem_limit_bytes=48 << 20
        ),
    )(*[
        pltpu.with_memory_space_constraint(a, pltpu.HBM)
        for a in (queries, keys, values, out_grad, state_in, exponents, boundaries)
    ])
    whole = jax.ShapeDtypeStruct((tokens, width), BF16)
    return pl.pallas_call(
        store,
        name="store",
        out_shape=(whole, whole, whole, jax.ShapeDtypeStruct((heads, srow, D), F32)),
        in_specs=[vmem] * 10,
        out_specs=(hbm,) * 4,
        scratch_shapes=[
            pltpu.VMEM((tokens, D), BF16),
            pltpu.VMEM((tokens, D), BF16),
            pltpu.SemaphoreType.DMA((12,)),
        ],
        compiler_params=pltpu.CompilerParams(vmem_limit_bytes=4 << 20),
    )(*results)


def solution(mesh):
    in_specs = (
        P("ctx", "head"),
        P("ctx", "head"),
        P("ctx", "head"),
        P(("ctx", "head"), None),
        P("head", None, None),
        P("head"),
        P(),
    )
    out_specs = (P("ctx", "head"), P("ctx", "head"), P("ctx", "head"), P("head", "ctx", None))
    return jax.shard_map(shards, mesh=mesh, in_specs=in_specs, out_specs=out_specs, check_vma=False)
```

```python
import functools

import jax
import jax.numpy as jnp
from jax import lax
from jax.experimental import pallas as pl
from jax.experimental.pallas import tpu as pltpu
from jax.sharding import PartitionSpec as P

D = 128
C = 256
MESH = pl.DeviceIdType.MESH
F32 = jnp.float32
BF16 = jnp.bfloat16
NN = ((1,), (0,))
NT = ((1,), (1,))


def dot(a, b, dims):
    return lax.dot_general(a, b, (dims, ((), ())), preferred_element_type=F32)


def far(step, size):
    return min(step, size - step)


def layer(
    sizes,
    q_hbm, k_hbm, v_hbm, og_hbm, st_hbm, exps_hbm, bnds_hbm,
    dq_ref, dk_ref, dv_ref, sg_ref, ki_ref, vi_ref, kl_ref, vl_ref, scale_ref, grad_ref,
    exps, bnds, q, k, v, g, st, ncol, nrow, tail, hin, w, wt, pk, qh,
    dqi, dki, dvi, prevs, nexts, edge_state,
    fs, fr, fo, fin, fins, bs, br, bo, bin_, bins,
    cs, cr, co, ci, gs_out, gs_in,
    segd, lastd, befored, afterd,
    lsem, gs, gr, fsem, bsem, csem, osem, ssem,
):
    heads, chunks, tokens, segments, nbounds, total = sizes
    groups = 16
    ctx = lax.axis_index("ctx")
    me = lax.axis_index("head")
    z, core = ctx // 2, ctx % 2
    y, x = me // 4, me % 4
    rows_each = tokens // groups
    width = heads * D
    srow = D // segments
    zs = segments // 2

    head_steps = sorted(
        [(a, b) for a in range(4) for b in range(4) if a or b],
        key=lambda s: -(far(s[0], 4) + far(s[1], 4)),
    )
    ctx_steps = sorted(
        [(a, b) for a in range(segments // 2) for b in range(2) if a or b],
        key=lambda s: -far(s[0], segments // 2),
    )

    def head_peer(step):
        return lax.rem(y + step[0], 4) * 4 + lax.rem(x + step[1], 4)

    def ctx_peer(step):
        return lax.rem(z + step[0], segments // 2) * 2 + lax.rem(core + step[1], 2)

    barrier = pltpu.get_barrier_semaphore()
    for s in ctx_steps:
        pl.semaphore_signal(barrier, inc=1, device_id=(ctx_peer(s), me), device_id_type=MESH)
    for s in head_steps:
        pl.semaphore_signal(barrier, inc=1, device_id=(ctx, head_peer(s)), device_id_type=MESH)

    loads = [
        pltpu.make_async_copy(k_hbm, k, lsem.at[0]),
        pltpu.make_async_copy(v_hbm, v, lsem.at[1]),
        pltpu.make_async_copy(q_hbm, q, lsem.at[2]),
        pltpu.make_async_copy(st_hbm.at[:, pl.ds(pl.multiple_of(ctx * srow, srow), srow), :], st, lsem.at[3]),
    ]
    smalls = [
        pltpu.make_async_copy(exps_hbm, exps, lsem.at[4]),
        pltpu.make_async_copy(bnds_hbm, bnds, lsem.at[5]),
    ]
    for c in smalls + loads:
        c.start()

    start = ctx * tokens

    def count(t):
        n = jnp.int32(0)
        for b in range(nbounds):
            n = n + jnp.where(bnds[b] <= t, 1, 0)
        return n.astype(F32)

    def rate(h):
        return exps[h].astype(F32) * (1.0 / (4.0 * total))

    def tile(value):
        return jnp.exp2(jnp.full((8, D), value, F32))

    def segment_decays(d, _):
        hits = count((d + 1) * tokens - 1) - count(d * tokens - 1)
        for h in range(heads):
            segd[h, d] = tile(-rate(h) * float(tokens) - hits)
        return 0

    def chunk_decays(c, _):
        low, high = count(start + c * C - 1), count(start + c * C + C - 1)
        first, end = count(start - 1), count(start + tokens - 1)
        passed = (c * C).astype(F32)
        for h in range(heads):
            lastd[h, c] = tile(-rate(h) * float(C) - (high - low))
            befored[h, c] = tile(-rate(h) * passed - (low - first))
            afterd[h, c] = tile(-rate(h) * (float(tokens - C) - passed) - (end - high))
        return 0

    def counts(c, _):
        first = start + c * C
        tc = first + lax.broadcasted_iota(jnp.int32, (C, D), 0)
        tr = first + lax.broadcasted_iota(jnp.int32, (8, C), 1)
        nc = jnp.zeros((C, D), F32)
        nr = jnp.zeros((8, C), F32)
        for b in range(nbounds):
            nc = nc + jnp.where(tc >= bnds[b], 1.0, 0.0)
            nr = nr + jnp.where(tr >= bnds[b], 1.0, 0.0)
        ncol[pl.ds(pl.multiple_of(c * C, C), C), :] = nc
        nrow[c] = nr
        return 0

    def rates(i, _):
        h, c = i // chunks, lax.rem(i, chunks)
        at = pl.ds(pl.multiple_of(c * C, C), C)
        a = rate(h)
        n = ncol[at, :]
        place = lax.broadcasted_iota(jnp.int32, (C, D), 0).astype(F32)
        before = count(start + c * C - 1)
        after = count(start + c * C + C - 1)
        hin[h, at, :] = jnp.exp2(-a * (place + 1.0) - (n - before))
        tail[h, at, :] = jnp.exp2(-a * ((C - 1.0) - place) - (after - n))
        return 0

    pl.semaphore_wait(barrier, len(head_steps) + len(ctx_steps))

    mine = pl.ds(pl.multiple_of(me * rows_each, rows_each), rows_each)
    def send_head(h, _):
        for s in head_steps:
            peer = head_peer(s)
            at = pl.multiple_of(peer * width + h * D, D)
            pltpu.make_async_remote_copy(
                src_ref=og_hbm.at[:, pl.ds(at, D)],
                dst_ref=g.at[mine, pl.ds(pl.multiple_of(h * D, D), D)],
                send_sem=gs,
                recv_sem=gr.at[h],
                device_id=(ctx, peer),
                device_id_type=MESH,
            ).start()
        return 0

    lax.fori_loop(0, heads, send_head, 0)
    for h in range(heads):
        at = pl.multiple_of(me * width + h * D, D)
        pltpu.make_async_copy(og_hbm.at[:, pl.ds(at, D)], g.at[mine, pl.ds(h * D, D)], gr.at[h]).start()

    for c in smalls:
        c.wait()
    lax.fori_loop(0, chunks, counts, 0)
    lax.fori_loop(0, heads * chunks, rates, 0)
    lax.fori_loop(0, chunks, chunk_decays, 0)
    lax.fori_loop(0, segments, segment_decays, 0)

    def exchange(src, dst, ssem, rsem):
        for s in ctx_steps:
            peer = ctx_peer(s)
            pltpu.make_async_remote_copy(
                src_ref=src.at[peer],
                dst_ref=dst.at[ctx],
                send_sem=ssem,
                recv_sem=rsem,
                device_id=(peer, me),
                device_id_type=MESH,
            ).start()
        dst[ctx] = src[ctx]

    def arrived(buf, sem):
        part = buf.at[pl.ds(0, segments - 1)]
        pltpu.make_async_copy(part, part, sem).wait()

    def seg_decay(lo, hi, d):
        return segd[lo:hi, d].reshape((hi - lo) * srow, D)

    def last(h, c):
        return lastd[h, c, 0:1, :]

    loads[0].wait()
    loads[1].wait()

    def own_forward(h, _):
        lanes = pl.ds(pl.multiple_of(h * D, D), D)

        def one(c, s):
            at = pl.ds(pl.multiple_of(c * C, C), C)
            kt = (k[at, lanes].astype(F32) * tail[h, at, :]).T.astype(BF16)
            prevs[h, c] = s
            return last(h, c) * s + dot(kt, v[at, lanes], NN)

        edge_state[h] = lax.fori_loop(0, chunks, one, jnp.zeros((D, D), F32), unroll=True)
        return 0

    lax.fori_loop(0, heads, own_forward, 0, unroll=True)

    def stage_forward(j, _):
        at = pl.ds(pl.multiple_of(j * srow, srow), srow)
        fs[j] = edge_state[:, at, :].reshape(heads * srow, D).astype(BF16)
        return 0

    lax.fori_loop(0, segments, stage_forward, 0)
    exchange(fs, fr, fsem.at[0], fsem.at[1])

    loads[2].wait()
    loads[3].wait()

    def prepare(i, _):
        h, c = i // chunks, lax.rem(i, chunks)
        at = pl.ds(pl.multiple_of(c * C, C), C)
        lanes = pl.ds(pl.multiple_of(h * D, D), D)
        a = rate(h)
        n = ncol[at, :]
        nc = jnp.concatenate([n, n], axis=1)
        nr = nrow[c][0:1, :]
        gap = (
            lax.broadcasted_iota(jnp.int32, (C, C), 0) - lax.broadcasted_iota(jnp.int32, (C, C), 1)
        ).astype(F32)
        dn = nc - nr
        w[i] = jnp.where(gap >= 0, jnp.exp2(-a * gap - dn), 0.0)
        weight = jnp.where(gap <= 0, jnp.exp2(a * gap + dn), 0.0)
        wt[i] = weight
        qc = q[at, lanes]
        pk[i] = (dot(k[at, lanes], qc, NT) * weight).astype(BF16)
        qh[i] = (qc.astype(F32) * hin[h, at, :]).T.astype(BF16)
        return 0

    lax.fori_loop(0, heads * chunks, prepare, 0, unroll=True)
    kl_ref[...] = k[:, (heads - 1) * D:]
    vl_ref[...] = v[:, (heads - 1) * D:]
    scale_ref[...] = tail[heads - 1]

    def own_backward(h):
        lanes = pl.ds(h * D, D)
        col = g.at[:, lanes]
        pltpu.make_async_copy(col, col, gr.at[h]).wait()

        def one(i, s):
            c = chunks - 1 - i
            at = pl.ds(pl.multiple_of(c * C, C), C)
            nexts[h, c] = s
            return last(h, c) * s + dot(qh[h * chunks + c], g[at, lanes], NN)

        edge_state[h] = lax.fori_loop(0, chunks, one, jnp.zeros((D, D), F32), unroll=True)

    def send_backward(p):
        def stage(j, _):
            at = pl.ds(pl.multiple_of(j * srow, srow), srow)
            bs[p, j] = edge_state[pl.ds(2 * p, 2), at, :].reshape(2 * srow, D).astype(BF16)
            return 0

        lax.fori_loop(0, segments, stage, 0)
        exchange(bs.at[p], br.at[p], bsem.at[p, 0], bsem.at[p, 1])

    def send_single(e):
        h = 2 + e
        cs[e] = edge_state[h].reshape(zs, D // zs, D).astype(BF16)

        def copy(to):
            return pltpu.make_async_remote_copy(
                src_ref=cs.at[e, to], dst_ref=cr.at[e, ctx], send_sem=csem.at[e, 0], recv_sem=csem.at[e, 1],
                device_id=(2 * to + e, me), device_id_type=MESH,
            )

        for step in sorted(range(1, zs), key=lambda n: -far(n, zs)):
            copy(lax.rem(z + step, zs)).start()

        @pl.when(core == e)
        def _():
            cr[e, ctx] = cs[e, z]

        @pl.when(core != e)
        def _():
            copy(z).start()

    def scan_single(e):
        h = 2 + e

        @pl.when(core == e)
        def _():
            arrived(cr.at[e], csem.at[e, 1])

            def one(i, s):
                d = segments - 1 - i
                co[d] = s.astype(BF16)
                return segd[h, d, 0:1, :] * s + cr[e, d].astype(F32)

            whole = lax.fori_loop(0, segments, one, jnp.zeros((D // zs, D), F32), unroll=True)
            for step in ctx_steps:
                peer = ctx_peer(step)
                pltpu.make_async_remote_copy(
                    src_ref=co.at[peer], dst_ref=ci.at[e, z], send_sem=osem.at[e, 0], recv_sem=osem.at[e, 1],
                    device_id=(peer, me), device_id_type=MESH,
                ).start()
            ci[e, z] = co[ctx]
            sg_ref[h] = whole[e * srow:(e + 1) * srow, :]
            gs_out[...] = whole[(1 - e) * srow:(2 - e) * srow, :]
            swap_rows().start()

    def swap_rows():
        return pltpu.make_async_remote_copy(
            src_ref=gs_out, dst_ref=gs_in, send_sem=ssem.at[0], recv_sem=ssem.at[1],
            device_id=(2 * z + 1 - core, me), device_id_type=MESH,
        )

    def slots(buf, n, sem):
        part = buf.at[pl.ds(0, n)]
        pltpu.make_async_copy(part, part, sem).wait()

    def join_single(e):
        @pl.when(core == e)
        def _():
            slots(ci.at[e], zs - 1, osem.at[e, 1])

        @pl.when(core != e)
        def _():
            slots(ci.at[e], zs, osem.at[e, 1])

        bins[2 + e] = ci[e].astype(F32).reshape(D, D)

    def end_single():
        swap_rows().wait()
        for e in range(2):
            @pl.when(core == e)
            def _():
                sg_ref[3 - e] = gs_in[...]
                slots(cs.at[e], zs - 1, csem.at[e, 0])
                slots(co, segments - 1, osem.at[e, 0])

            @pl.when(core != e)
            def _():
                slots(cs.at[e], zs, csem.at[e, 0])

    def scan_forward():
        arrived(fr, fsem.at[1])

        def one(d, s):
            fo[d] = s.astype(BF16)
            return seg_decay(0, heads, d) * s + fr[d].astype(F32)

        lax.fori_loop(0, segments, one, st[...].reshape(heads * srow, D), unroll=True)
        exchange(fo, fin, fsem.at[2], fsem.at[3])

    def scan_backward(p):
        arrived(br.at[p], bsem.at[p, 1])

        def one(i, s):
            d = segments - 1 - i
            bo[p, d] = s.astype(BF16)
            return seg_decay(2 * p, 2 * p + 2, d) * s + br[p, d].astype(F32)

        whole = lax.fori_loop(0, segments, one, jnp.zeros((2 * srow, D), F32), unroll=True)
        sg_ref[pl.ds(2 * p, 2)] = whole.reshape(2, srow, D)
        exchange(bo.at[p], bin_.at[p], bsem.at[p, 2], bsem.at[p, 3])

    def inside(h):
        lanes = pl.ds(h * D, D)

        def one(c, _):
            at = pl.ds(pl.multiple_of(c * C, C), C)
            i = h * chunks + c
            gc, vc = g[at, lanes], v[at, lanes]
            grad = (dot(gc, vc, NT) * w[i]).astype(BF16)
            dqi[at, lanes] = dot(grad, k[at, lanes], NN)
            turned = (dot(vc, gc, NT) * wt[i]).astype(BF16)
            dk_part, dv_part = dot(turned, q[at, lanes], NN), dot(pk[i], gc, NN)
            if h == heads - 1:
                ki_ref[at, :] = dk_part
                vi_ref[at, :] = dv_part
            else:
                dki[at, lanes] = dk_part
                dvi[at, lanes] = dv_part
            return 0

        lax.fori_loop(0, chunks, one, 0, unroll=True)

    def finish_query():
        arrived(fin, fsem.at[3])
        got = fin[...].astype(F32)
        for h in range(heads):
            fins[h] = got[:, h * srow:(h + 1) * srow, :].reshape(D, D)

        def one(i, _):
            h, c = i // chunks, lax.rem(i, chunks)
            at = pl.ds(pl.multiple_of(c * C, C), C)
            lanes = pl.ds(pl.multiple_of(h * D, D), D)
            state = (prevs[h, c] + befored[h, c, 0:1, :] * fins[h]).astype(BF16)
            dq_ref[at, lanes] = (dqi[at, lanes] + hin[h, at, :] * dot(g[at, lanes], state, NT)).astype(BF16)
            return 0

        lax.fori_loop(0, heads * chunks, one, 0, unroll=True)

    def join_pair(p):
        arrived(bin_.at[p], bsem.at[p, 3])
        got = bin_[p].astype(F32)
        for e in range(2):
            bins[2 * p + e] = got[:, e * srow:(e + 1) * srow, :].reshape(D, D)

    def finish_keys(h):
        lanes = pl.ds(h * D, D)

        def one(c, _):
            at = pl.ds(pl.multiple_of(c * C, C), C)
            grad = (nexts[h, c] + afterd[h, c, 0:1, :] * bins[h]).astype(BF16)
            scale = tail[h, at, :]
            dk_ref[at, lanes] = (dki[at, lanes] + scale * dot(v[at, lanes], grad, NT)).astype(BF16)
            dv_ref[at, lanes] = (dvi[at, lanes] + scale * dot(k[at, lanes], grad, NN)).astype(BF16)
            return 0

        lax.fori_loop(0, chunks, one, 0, unroll=True)

    own_backward(0)
    inside(0)
    own_backward(1)
    send_backward(0)
    scan_forward()
    inside(1)
    own_backward(2)
    send_single(0)
    scan_backward(0)
    own_backward(3)
    send_single(1)
    scan_single(0)
    inside(2)
    inside(3)
    scan_single(1)
    finish_query()
    join_pair(0)
    finish_keys(0)
    finish_keys(1)
    join_single(0)
    finish_keys(2)
    sent = og_hbm.at[:, pl.ds(0, (groups - 1) * width)]
    pltpu.make_async_copy(sent, sent, gs).wait()
    arrived(fs, fsem.at[0])
    arrived(fo, fsem.at[2])
    arrived(bs.at[0], bsem.at[0, 0])
    arrived(bo.at[0], bsem.at[0, 2])
    end_single()
    join_single(1)
    for c in range(chunks):
        grad_ref[c] = (nexts[heads - 1, c] + afterd[heads - 1, c, 0:1, :] * bins[heads - 1]).astype(BF16)


def store(dq, dk, dv, sg, ki, vi, kl, vl, scale, grad, dq_hbm, dk_hbm, dv_hbm, sg_hbm, lk, lv, sem):
    rows = dq.shape[0] // 4
    done = dk.shape[1] - D
    copies = [pltpu.make_async_copy(dq, dq_hbm, sem.at[0]), pltpu.make_async_copy(sg, sg_hbm, sem.at[1])]
    for j, (src, dst) in enumerate(((dk, dk_hbm), (dv, dv_hbm))):
        first = pl.ds(0, done)
        copies.append(pltpu.make_async_copy(src.at[:, first], dst.at[:, first], sem.at[2 + j]))
    for copy in copies:
        copy.start()
    for c in range(4):
        at = pl.ds(c * rows, rows)
        for j, (part, other, dims, last, dst) in enumerate(
            ((ki, vl, NT, lk, dk_hbm), (vi, kl, NN, lv, dv_hbm))
        ):
            last[at, :] = (part[at, :] + scale[at, :] * dot(other[at, :], grad[c], dims)).astype(BF16)
            copy = pltpu.make_async_copy(last.at[at], dst.at[at, pl.ds(done, D)], sem.at[4 + 2 * c + j])
            copy.start()
            copies.append(copy)
    for copy in copies:
        copy.wait()


def shards(queries, keys, values, out_grad, state_in, exponents, boundaries):
    tokens, width = queries.shape
    heads = width // D
    chunks = tokens // C
    segments = lax.axis_size("ctx")
    srow = D // segments
    total = tokens * segments
    sizes = (heads, chunks, tokens, segments, boundaries.shape[0], total)
    hbm = pl.BlockSpec(memory_space=pltpu.HBM)
    vmem = pl.BlockSpec(memory_space=pltpu.VMEM)
    n = heads * chunks
    slab = lambda rows: pltpu.VMEM((segments, rows, D), BF16)
    pair = lambda: pltpu.VMEM((1, segments, 2 * srow, D), BF16)
    results = pl.pallas_call(
        functools.partial(layer, sizes),
        name="layer",
        out_shape=(
            pltpu.VMEM((tokens, width), BF16),
            pltpu.VMEM((tokens, width), BF16),
            pltpu.VMEM((tokens, width), BF16),
            pltpu.VMEM((heads, srow, D), F32),
            pltpu.VMEM((tokens, D), F32),
            pltpu.VMEM((tokens, D), F32),
            pltpu.VMEM((tokens, D), BF16),
            pltpu.VMEM((tokens, D), BF16),
            pltpu.VMEM((tokens, D), F32),
            pltpu.VMEM((chunks, D, D), BF16),
        ),
        in_specs=[hbm] * 7,
        out_specs=(vmem,) * 10,
        scratch_shapes=[
            pltpu.SMEM((heads,), jnp.int32),
            pltpu.SMEM((boundaries.shape[0],), jnp.int32),
            pltpu.VMEM((tokens, width), BF16),
            pltpu.VMEM((tokens, width), BF16),
            pltpu.VMEM((tokens, width), BF16),
            pltpu.VMEM((tokens, width), BF16),
            pltpu.VMEM((heads, srow, D), F32),
            pltpu.VMEM((tokens, D), F32),
            pltpu.VMEM((chunks, 8, C), F32),
            pltpu.VMEM((heads, tokens, D), F32),
            pltpu.VMEM((heads, tokens, D), F32),
            pltpu.VMEM((n, C, C), F32),
            pltpu.VMEM((n, C, C), F32),
            pltpu.VMEM((n, C, C), BF16),
            pltpu.VMEM((n, D, C), BF16),
            pltpu.VMEM((tokens, width), F32),
            pltpu.VMEM((tokens, width), F32),
            pltpu.VMEM((tokens, width), F32),
            pltpu.VMEM((heads, chunks, D, D), F32),
            pltpu.VMEM((heads, chunks, D, D), F32),
            pltpu.VMEM((heads, D, D), F32),
            slab(heads * srow),
            slab(heads * srow),
            slab(heads * srow),
            slab(heads * srow),
            pltpu.VMEM((heads, D, D), F32),
            pair(),
            pair(),
            pair(),
            pair(),
            pltpu.VMEM((heads, D, D), F32),
            pltpu.VMEM((2, segments // 2, 2 * srow, D), BF16),
            pltpu.VMEM((2, segments, 2 * srow, D), BF16),
            pltpu.VMEM((segments, 2 * srow, D), BF16),
            pltpu.VMEM((2, segments // 2, 2 * srow, D), BF16),
            pltpu.VMEM((srow, D), F32),
            pltpu.VMEM((srow, D), F32),
            pltpu.VMEM((heads, segments, 8, D), F32),
            pltpu.VMEM((heads, chunks, 8, D), F32),
            pltpu.VMEM((heads, chunks, 8, D), F32),
            pltpu.VMEM((heads, chunks, 8, D), F32),
            pltpu.SemaphoreType.DMA((6,)),
            pltpu.SemaphoreType.DMA,
            pltpu.SemaphoreType.DMA((heads,)),
            pltpu.SemaphoreType.DMA((4,)),
            pltpu.SemaphoreType.DMA((1, 4)),
            pltpu.SemaphoreType.DMA((2, 2)),
            pltpu.SemaphoreType.DMA((2, 2)),
            pltpu.SemaphoreType.DMA((2,)),
        ],
        compiler_params=pltpu.CompilerParams(
            collective_id=0, has_side_effects=True, vmem_limit_bytes=48 << 20
        ),
    )(*[
        pltpu.with_memory_space_constraint(a, pltpu.HBM)
        for a in (queries, keys, values, out_grad, state_in, exponents, boundaries)
    ])
    whole = jax.ShapeDtypeStruct((tokens, width), BF16)
    return pl.pallas_call(
        store,
        name="store",
        out_shape=(whole, whole, whole, jax.ShapeDtypeStruct((heads, srow, D), F32)),
        in_specs=[vmem] * 10,
        out_specs=(hbm,) * 4,
        scratch_shapes=[
            pltpu.VMEM((tokens, D), BF16),
            pltpu.VMEM((tokens, D), BF16),
            pltpu.SemaphoreType.DMA((12,)),
        ],
        compiler_params=pltpu.CompilerParams(vmem_limit_bytes=4 << 20),
    )(*results)


def solution(mesh):
    in_specs = (
        P("ctx", "head"),
        P("ctx", "head"),
        P("ctx", "head"),
        P(("ctx", "head"), None),
        P("head", None, None),
        P("head"),
        P(),
    )
    out_specs = (P("ctx", "head"), P("ctx", "head"), P("ctx", "head"), P("head", "ctx", None))
    return jax.shard_map(shards, mesh=mesh, in_specs=in_specs, out_specs=out_specs, check_vma=False)
```

```python
import functools

import jax
import jax.numpy as jnp
from jax import lax
from jax.experimental import pallas as pl
from jax.experimental.pallas import tpu as pltpu
from jax.sharding import PartitionSpec as P

D = 128
C = 256
MESH = pl.DeviceIdType.MESH
F32 = jnp.float32
BF16 = jnp.bfloat16
NN = ((1,), (0,))
NT = ((1,), (1,))


def dot(a, b, dims):
    return lax.dot_general(a, b, (dims, ((), ())), preferred_element_type=F32)


def far(step, size):
    return min(step, size - step)


def layer(
    sizes,
    q_hbm, k_hbm, v_hbm, og_hbm, st_hbm, exps_hbm, bnds_hbm,
    dq_ref, dk_ref, dv_ref, sg_ref, ki_ref, vi_ref, kl_ref, vl_ref, scale_ref, grad_ref,
    exps, bnds, q, k, v, g, st, ncol, nrow, tail, hin, w, wt, pk, qh,
    dqi, dki, dvi, prevs, nexts, edge_state,
    fs, fr, fo, fin, fins, bs, br, bo, bin_, bins,
    cs, cr, co, ci, gs_out, gs_in,
    segd, lastd, befored, afterd,
    lsem, gs, gr, fsem, bsem, csem, osem, ssem,
):
    heads, chunks, tokens, segments, nbounds, total = sizes
    groups = 16
    ctx = lax.axis_index("ctx")
    me = lax.axis_index("head")
    z, core = ctx // 2, ctx % 2
    y, x = me // 4, me % 4
    rows_each = tokens // groups
    width = heads * D
    srow = D // segments
    zs = segments // 2

    head_steps = sorted(
        [(a, b) for a in range(4) for b in range(4) if a or b],
        key=lambda s: -(far(s[0], 4) + far(s[1], 4)),
    )
    ctx_steps = sorted(
        [(a, b) for a in range(segments // 2) for b in range(2) if a or b],
        key=lambda s: -far(s[0], segments // 2),
    )

    def head_peer(step):
        return lax.rem(y + step[0], 4) * 4 + lax.rem(x + step[1], 4)

    def ctx_peer(step):
        return lax.rem(z + step[0], segments // 2) * 2 + lax.rem(core + step[1], 2)

    barrier = pltpu.get_barrier_semaphore()
    for s in ctx_steps:
        pl.semaphore_signal(barrier, inc=1, device_id=(ctx_peer(s), me), device_id_type=MESH)
    for s in head_steps:
        pl.semaphore_signal(barrier, inc=1, device_id=(ctx, head_peer(s)), device_id_type=MESH)

    loads = [
        pltpu.make_async_copy(k_hbm, k, lsem.at[0]),
        pltpu.make_async_copy(v_hbm, v, lsem.at[1]),
        pltpu.make_async_copy(q_hbm, q, lsem.at[2]),
        pltpu.make_async_copy(st_hbm.at[:, pl.ds(pl.multiple_of(ctx * srow, srow), srow), :], st, lsem.at[3]),
    ]
    smalls = [
        pltpu.make_async_copy(exps_hbm, exps, lsem.at[4]),
        pltpu.make_async_copy(bnds_hbm, bnds, lsem.at[5]),
    ]
    for c in smalls + loads:
        c.start()

    start = ctx * tokens

    def count(t):
        n = jnp.int32(0)
        for b in range(nbounds):
            n = n + jnp.where(bnds[b] <= t, 1, 0)
        return n.astype(F32)

    def rate(h):
        return exps[h].astype(F32) * (1.0 / (4.0 * total))

    def tile(value):
        return jnp.exp2(jnp.full((8, D), value, F32))

    def segment_decays(d, _):
        hits = count((d + 1) * tokens - 1) - count(d * tokens - 1)
        for h in range(heads):
            segd[h, d] = tile(-rate(h) * float(tokens) - hits)
        return 0

    def chunk_decays(c, _):
        low, high = count(start + c * C - 1), count(start + c * C + C - 1)
        first, end = count(start - 1), count(start + tokens - 1)
        passed = (c * C).astype(F32)
        for h in range(heads):
            lastd[h, c] = tile(-rate(h) * float(C) - (high - low))
            befored[h, c] = tile(-rate(h) * passed - (low - first))
            afterd[h, c] = tile(-rate(h) * (float(tokens - C) - passed) - (end - high))
        return 0

    def counts(c, _):
        first = start + c * C
        tc = first + lax.broadcasted_iota(jnp.int32, (C, D), 0)
        tr = first + lax.broadcasted_iota(jnp.int32, (8, C), 1)
        nc = jnp.zeros((C, D), F32)
        nr = jnp.zeros((8, C), F32)
        for b in range(nbounds):
            nc = nc + jnp.where(tc >= bnds[b], 1.0, 0.0)
            nr = nr + jnp.where(tr >= bnds[b], 1.0, 0.0)
        ncol[pl.ds(pl.multiple_of(c * C, C), C), :] = nc
        nrow[c] = nr
        return 0

    def rates(i, _):
        h, c = i // chunks, lax.rem(i, chunks)
        at = pl.ds(pl.multiple_of(c * C, C), C)
        a = rate(h)
        n = ncol[at, :]
        place = lax.broadcasted_iota(jnp.int32, (C, D), 0).astype(F32)
        before = count(start + c * C - 1)
        after = count(start + c * C + C - 1)
        hin[h, at, :] = jnp.exp2(-a * (place + 1.0) - (n - before))
        tail[h, at, :] = jnp.exp2(-a * ((C - 1.0) - place) - (after - n))
        return 0

    pl.semaphore_wait(barrier, len(head_steps) + len(ctx_steps))

    mine = pl.ds(pl.multiple_of(me * rows_each, rows_each), rows_each)
    def send_head(h, _):
        for s in head_steps:
            peer = head_peer(s)
            at = pl.multiple_of(peer * width + h * D, D)
            pltpu.make_async_remote_copy(
                src_ref=og_hbm.at[:, pl.ds(at, D)],
                dst_ref=g.at[mine, pl.ds(pl.multiple_of(h * D, D), D)],
                send_sem=gs,
                recv_sem=gr.at[h],
                device_id=(ctx, peer),
                device_id_type=MESH,
            ).start()
        return 0

    lax.fori_loop(0, heads, send_head, 0)
    for h in range(heads):
        at = pl.multiple_of(me * width + h * D, D)
        pltpu.make_async_copy(og_hbm.at[:, pl.ds(at, D)], g.at[mine, pl.ds(h * D, D)], gr.at[h]).start()

    for c in smalls:
        c.wait()
    lax.fori_loop(0, chunks, counts, 0)
    lax.fori_loop(0, heads * chunks, rates, 0)
    lax.fori_loop(0, chunks, chunk_decays, 0)
    lax.fori_loop(0, segments, segment_decays, 0)

    def exchange(src, dst, ssem, rsem):
        for s in ctx_steps:
            peer = ctx_peer(s)
            pltpu.make_async_remote_copy(
                src_ref=src.at[peer],
                dst_ref=dst.at[ctx],
                send_sem=ssem,
                recv_sem=rsem,
                device_id=(peer, me),
                device_id_type=MESH,
            ).start()
        dst[ctx] = src[ctx]

    def arrived(buf, sem):
        part = buf.at[pl.ds(0, segments - 1)]
        pltpu.make_async_copy(part, part, sem).wait()

    def seg_decay(lo, hi, d):
        return segd[lo:hi, d].reshape((hi - lo) * srow, D)

    def last(h, c):
        return lastd[h, c, 0:1, :]

    loads[0].wait()
    loads[1].wait()

    def own_forward(h, _):
        lanes = pl.ds(pl.multiple_of(h * D, D), D)

        def one(c, s):
            at = pl.ds(pl.multiple_of(c * C, C), C)
            kt = (k[at, lanes].astype(F32) * tail[h, at, :]).T.astype(BF16)
            prevs[h, c] = s
            return last(h, c) * s + dot(kt, v[at, lanes], NN)

        edge_state[h] = lax.fori_loop(0, chunks, one, jnp.zeros((D, D), F32), unroll=True)
        return 0

    lax.fori_loop(0, heads, own_forward, 0, unroll=True)

    def stage_forward(j, _):
        at = pl.ds(pl.multiple_of(j * srow, srow), srow)
        fs[j] = edge_state[:, at, :].reshape(heads * srow, D).astype(BF16)
        return 0

    lax.fori_loop(0, segments, stage_forward, 0)
    exchange(fs, fr, fsem.at[0], fsem.at[1])

    loads[2].wait()
    loads[3].wait()

    def prepare(i, _):
        h, c = i // chunks, lax.rem(i, chunks)
        at = pl.ds(pl.multiple_of(c * C, C), C)
        lanes = pl.ds(pl.multiple_of(h * D, D), D)
        a = rate(h)
        n = ncol[at, :]
        nc = jnp.concatenate([n, n], axis=1)
        nr = nrow[c][0:1, :]
        gap = (
            lax.broadcasted_iota(jnp.int32, (C, C), 0) - lax.broadcasted_iota(jnp.int32, (C, C), 1)
        ).astype(F32)
        dn = nc - nr
        w[i] = jnp.where(gap >= 0, jnp.exp2(-a * gap - dn), 0.0)
        weight = jnp.where(gap <= 0, jnp.exp2(a * gap + dn), 0.0)
        wt[i] = weight
        qc = q[at, lanes]
        pk[i] = (dot(k[at, lanes], qc, NT) * weight).astype(BF16)
        qh[i] = (qc.astype(F32) * hin[h, at, :]).T.astype(BF16)
        return 0

    lax.fori_loop(0, heads * chunks, prepare, 0, unroll=4)
    kl_ref[...] = k[:, (heads - 1) * D:]
    vl_ref[...] = v[:, (heads - 1) * D:]
    scale_ref[...] = tail[heads - 1]

    def own_backward(h):
        lanes = pl.ds(h * D, D)
        col = g.at[:, lanes]
        pltpu.make_async_copy(col, col, gr.at[h]).wait()

        def one(i, s):
            c = chunks - 1 - i
            at = pl.ds(pl.multiple_of(c * C, C), C)
            nexts[h, c] = s
            return last(h, c) * s + dot(qh[h * chunks + c], g[at, lanes], NN)

        edge_state[h] = lax.fori_loop(0, chunks, one, jnp.zeros((D, D), F32), unroll=True)

    def send_backward(p):
        def stage(j, _):
            at = pl.ds(pl.multiple_of(j * srow, srow), srow)
            bs[p, j] = edge_state[pl.ds(2 * p, 2), at, :].reshape(2 * srow, D).astype(BF16)
            return 0

        lax.fori_loop(0, segments, stage, 0)
        exchange(bs.at[p], br.at[p], bsem.at[p, 0], bsem.at[p, 1])

    def send_single(e):
        h = 2 + e
        cs[e] = edge_state[h].reshape(zs, D // zs, D).astype(BF16)

        def copy(to):
            return pltpu.make_async_remote_copy(
                src_ref=cs.at[e, to], dst_ref=cr.at[e, ctx], send_sem=csem.at[e, 0], recv_sem=csem.at[e, 1],
                device_id=(2 * to + e, me), device_id_type=MESH,
            )

        for step in sorted(range(1, zs), key=lambda n: -far(n, zs)):
            copy(lax.rem(z + step, zs)).start()

        @pl.when(core == e)
        def _():
            cr[e, ctx] = cs[e, z]

        @pl.when(core != e)
        def _():
            copy(z).start()

    def scan_single(e):
        h = 2 + e

        @pl.when(core == e)
        def _():
            arrived(cr.at[e], csem.at[e, 1])

            def one(i, s):
                d = segments - 1 - i
                co[d] = s.astype(BF16)
                return segd[h, d, 0:1, :] * s + cr[e, d].astype(F32)

            whole = lax.fori_loop(0, segments, one, jnp.zeros((D // zs, D), F32), unroll=True)
            for step in ctx_steps:
                peer = ctx_peer(step)
                pltpu.make_async_remote_copy(
                    src_ref=co.at[peer], dst_ref=ci.at[e, z], send_sem=osem.at[e, 0], recv_sem=osem.at[e, 1],
                    device_id=(peer, me), device_id_type=MESH,
                ).start()
            ci[e, z] = co[ctx]
            sg_ref[h] = whole[e * srow:(e + 1) * srow, :]
            gs_out[...] = whole[(1 - e) * srow:(2 - e) * srow, :]
            swap_rows().start()

    def swap_rows():
        return pltpu.make_async_remote_copy(
            src_ref=gs_out, dst_ref=gs_in, send_sem=ssem.at[0], recv_sem=ssem.at[1],
            device_id=(2 * z + 1 - core, me), device_id_type=MESH,
        )

    def slots(buf, n, sem):
        part = buf.at[pl.ds(0, n)]
        pltpu.make_async_copy(part, part, sem).wait()

    def join_single(e):
        @pl.when(core == e)
        def _():
            slots(ci.at[e], zs - 1, osem.at[e, 1])

        @pl.when(core != e)
        def _():
            slots(ci.at[e], zs, osem.at[e, 1])

        bins[2 + e] = ci[e].astype(F32).reshape(D, D)

    def end_single():
        swap_rows().wait()
        for e in range(2):
            @pl.when(core == e)
            def _():
                sg_ref[3 - e] = gs_in[...]
                slots(cs.at[e], zs - 1, csem.at[e, 0])
                slots(co, segments - 1, osem.at[e, 0])

            @pl.when(core != e)
            def _():
                slots(cs.at[e], zs, csem.at[e, 0])

    def scan_forward():
        arrived(fr, fsem.at[1])

        def one(d, s):
            fo[d] = s.astype(BF16)
            return seg_decay(0, heads, d) * s + fr[d].astype(F32)

        lax.fori_loop(0, segments, one, st[...].reshape(heads * srow, D), unroll=True)
        exchange(fo, fin, fsem.at[2], fsem.at[3])

    def scan_backward(p):
        arrived(br.at[p], bsem.at[p, 1])

        def one(i, s):
            d = segments - 1 - i
            bo[p, d] = s.astype(BF16)
            return seg_decay(2 * p, 2 * p + 2, d) * s + br[p, d].astype(F32)

        whole = lax.fori_loop(0, segments, one, jnp.zeros((2 * srow, D), F32), unroll=True)
        sg_ref[pl.ds(2 * p, 2)] = whole.reshape(2, srow, D)
        exchange(bo.at[p], bin_.at[p], bsem.at[p, 2], bsem.at[p, 3])

    def inside(h):
        lanes = pl.ds(h * D, D)

        def one(c, _):
            at = pl.ds(pl.multiple_of(c * C, C), C)
            i = h * chunks + c
            gc, vc = g[at, lanes], v[at, lanes]
            grad = (dot(gc, vc, NT) * w[i]).astype(BF16)
            dqi[at, lanes] = dot(grad, k[at, lanes], NN)
            turned = (dot(vc, gc, NT) * wt[i]).astype(BF16)
            dk_part, dv_part = dot(turned, q[at, lanes], NN), dot(pk[i], gc, NN)
            if h == heads - 1:
                ki_ref[at, :] = dk_part
                vi_ref[at, :] = dv_part
            else:
                dki[at, lanes] = dk_part
                dvi[at, lanes] = dv_part
            return 0

        lax.fori_loop(0, chunks, one, 0, unroll=True)

    def finish_query():
        arrived(fin, fsem.at[3])
        got = fin[...].astype(F32)
        for h in range(heads):
            fins[h] = got[:, h * srow:(h + 1) * srow, :].reshape(D, D)

        def one(i, _):
            h, c = i // chunks, lax.rem(i, chunks)
            at = pl.ds(pl.multiple_of(c * C, C), C)
            lanes = pl.ds(pl.multiple_of(h * D, D), D)
            state = (prevs[h, c] + befored[h, c, 0:1, :] * fins[h]).astype(BF16)
            dq_ref[at, lanes] = (dqi[at, lanes] + hin[h, at, :] * dot(g[at, lanes], state, NT)).astype(BF16)
            return 0

        lax.fori_loop(0, heads * chunks, one, 0, unroll=True)

    def join_pair(p):
        arrived(bin_.at[p], bsem.at[p, 3])
        got = bin_[p].astype(F32)
        for e in range(2):
            bins[2 * p + e] = got[:, e * srow:(e + 1) * srow, :].reshape(D, D)

    def finish_keys(h):
        lanes = pl.ds(h * D, D)

        def one(c, _):
            at = pl.ds(pl.multiple_of(c * C, C), C)
            grad = (nexts[h, c] + afterd[h, c, 0:1, :] * bins[h]).astype(BF16)
            scale = tail[h, at, :]
            dk_ref[at, lanes] = (dki[at, lanes] + scale * dot(v[at, lanes], grad, NT)).astype(BF16)
            dv_ref[at, lanes] = (dvi[at, lanes] + scale * dot(k[at, lanes], grad, NN)).astype(BF16)
            return 0

        lax.fori_loop(0, chunks, one, 0, unroll=True)

    own_backward(0)
    inside(0)
    own_backward(1)
    send_backward(0)
    scan_forward()
    inside(1)
    own_backward(2)
    send_single(0)
    scan_backward(0)
    own_backward(3)
    send_single(1)
    scan_single(0)
    inside(2)
    inside(3)
    scan_single(1)
    finish_query()
    join_pair(0)
    finish_keys(0)
    finish_keys(1)
    join_single(0)
    finish_keys(2)
    sent = og_hbm.at[:, pl.ds(0, (groups - 1) * width)]
    pltpu.make_async_copy(sent, sent, gs).wait()
    arrived(fs, fsem.at[0])
    arrived(fo, fsem.at[2])
    arrived(bs.at[0], bsem.at[0, 0])
    arrived(bo.at[0], bsem.at[0, 2])
    end_single()
    join_single(1)
    for c in range(chunks):
        grad_ref[c] = (nexts[heads - 1, c] + afterd[heads - 1, c, 0:1, :] * bins[heads - 1]).astype(BF16)


def store(dq, dk, dv, sg, ki, vi, kl, vl, scale, grad, dq_hbm, dk_hbm, dv_hbm, sg_hbm, lk, lv, sem):
    rows = dq.shape[0] // 4
    done = dk.shape[1] - D
    copies = [pltpu.make_async_copy(dq, dq_hbm, sem.at[0]), pltpu.make_async_copy(sg, sg_hbm, sem.at[1])]
    for j, (src, dst) in enumerate(((dk, dk_hbm), (dv, dv_hbm))):
        first = pl.ds(0, done)
        copies.append(pltpu.make_async_copy(src.at[:, first], dst.at[:, first], sem.at[2 + j]))
    for copy in copies:
        copy.start()
    for c in range(4):
        at = pl.ds(c * rows, rows)
        for j, (part, other, dims, last, dst) in enumerate(
            ((ki, vl, NT, lk, dk_hbm), (vi, kl, NN, lv, dv_hbm))
        ):
            last[at, :] = (part[at, :] + scale[at, :] * dot(other[at, :], grad[c], dims)).astype(BF16)
            copy = pltpu.make_async_copy(last.at[at], dst.at[at, pl.ds(done, D)], sem.at[4 + 2 * c + j])
            copy.start()
            copies.append(copy)
    for copy in copies:
        copy.wait()


def shards(queries, keys, values, out_grad, state_in, exponents, boundaries):
    tokens, width = queries.shape
    heads = width // D
    chunks = tokens // C
    segments = lax.axis_size("ctx")
    srow = D // segments
    total = tokens * segments
    sizes = (heads, chunks, tokens, segments, boundaries.shape[0], total)
    hbm = pl.BlockSpec(memory_space=pltpu.HBM)
    vmem = pl.BlockSpec(memory_space=pltpu.VMEM)
    n = heads * chunks
    slab = lambda rows: pltpu.VMEM((segments, rows, D), BF16)
    pair = lambda: pltpu.VMEM((1, segments, 2 * srow, D), BF16)
    results = pl.pallas_call(
        functools.partial(layer, sizes),
        name="layer",
        out_shape=(
            pltpu.VMEM((tokens, width), BF16),
            pltpu.VMEM((tokens, width), BF16),
            pltpu.VMEM((tokens, width), BF16),
            pltpu.VMEM((heads, srow, D), F32),
            pltpu.VMEM((tokens, D), F32),
            pltpu.VMEM((tokens, D), F32),
            pltpu.VMEM((tokens, D), BF16),
            pltpu.VMEM((tokens, D), BF16),
            pltpu.VMEM((tokens, D), F32),
            pltpu.VMEM((chunks, D, D), BF16),
        ),
        in_specs=[hbm] * 7,
        out_specs=(vmem,) * 10,
        scratch_shapes=[
            pltpu.SMEM((heads,), jnp.int32),
            pltpu.SMEM((boundaries.shape[0],), jnp.int32),
            pltpu.VMEM((tokens, width), BF16),
            pltpu.VMEM((tokens, width), BF16),
            pltpu.VMEM((tokens, width), BF16),
            pltpu.VMEM((tokens, width), BF16),
            pltpu.VMEM((heads, srow, D), F32),
            pltpu.VMEM((tokens, D), F32),
            pltpu.VMEM((chunks, 8, C), F32),
            pltpu.VMEM((heads, tokens, D), F32),
            pltpu.VMEM((heads, tokens, D), F32),
            pltpu.VMEM((n, C, C), F32),
            pltpu.VMEM((n, C, C), F32),
            pltpu.VMEM((n, C, C), BF16),
            pltpu.VMEM((n, D, C), BF16),
            pltpu.VMEM((tokens, width), F32),
            pltpu.VMEM((tokens, width), F32),
            pltpu.VMEM((tokens, width), F32),
            pltpu.VMEM((heads, chunks, D, D), F32),
            pltpu.VMEM((heads, chunks, D, D), F32),
            pltpu.VMEM((heads, D, D), F32),
            slab(heads * srow),
            slab(heads * srow),
            slab(heads * srow),
            slab(heads * srow),
            pltpu.VMEM((heads, D, D), F32),
            pair(),
            pair(),
            pair(),
            pair(),
            pltpu.VMEM((heads, D, D), F32),
            pltpu.VMEM((2, segments // 2, 2 * srow, D), BF16),
            pltpu.VMEM((2, segments, 2 * srow, D), BF16),
            pltpu.VMEM((segments, 2 * srow, D), BF16),
            pltpu.VMEM((2, segments // 2, 2 * srow, D), BF16),
            pltpu.VMEM((srow, D), F32),
            pltpu.VMEM((srow, D), F32),
            pltpu.VMEM((heads, segments, 8, D), F32),
            pltpu.VMEM((heads, chunks, 8, D), F32),
            pltpu.VMEM((heads, chunks, 8, D), F32),
            pltpu.VMEM((heads, chunks, 8, D), F32),
            pltpu.SemaphoreType.DMA((6,)),
            pltpu.SemaphoreType.DMA,
            pltpu.SemaphoreType.DMA((heads,)),
            pltpu.SemaphoreType.DMA((4,)),
            pltpu.SemaphoreType.DMA((1, 4)),
            pltpu.SemaphoreType.DMA((2, 2)),
            pltpu.SemaphoreType.DMA((2, 2)),
            pltpu.SemaphoreType.DMA((2,)),
        ],
        compiler_params=pltpu.CompilerParams(
            collective_id=0, has_side_effects=True, vmem_limit_bytes=48 << 20
        ),
    )(*[
        pltpu.with_memory_space_constraint(a, pltpu.HBM)
        for a in (queries, keys, values, out_grad, state_in, exponents, boundaries)
    ])
    whole = jax.ShapeDtypeStruct((tokens, width), BF16)
    return pl.pallas_call(
        store,
        name="store",
        out_shape=(whole, whole, whole, jax.ShapeDtypeStruct((heads, srow, D), F32)),
        in_specs=[vmem] * 10,
        out_specs=(hbm,) * 4,
        scratch_shapes=[
            pltpu.VMEM((tokens, D), BF16),
            pltpu.VMEM((tokens, D), BF16),
            pltpu.SemaphoreType.DMA((12,)),
        ],
        compiler_params=pltpu.CompilerParams(vmem_limit_bytes=4 << 20),
    )(*results)


def solution(mesh):
    in_specs = (
        P("ctx", "head"),
        P("ctx", "head"),
        P("ctx", "head"),
        P(("ctx", "head"), None),
        P("head", None, None),
        P("head"),
        P(),
    )
    out_specs = (P("ctx", "head"), P("ctx", "head"), P("ctx", "head"), P("head", "ctx", None))
    return jax.shard_map(shards, mesh=mesh, in_specs=in_specs, out_specs=out_specs, check_vma=False)
```
